128 devices in a mesh: ctx: 16 (over x_lo, z, core), exp: 8 (over y, x_hi).
Axes of the slice: x: 4 (x_hi: 2, x_lo: 2; x = x_hi * 2 + x_lo), y: 4, z: 4, core: 2. Of those that a mesh axis runs over, the one named last changes fastest.
Arguments:
- stream: bfloat16 [16384, 2048], P(('ctx', 'exp')), may hold values from -4 to 4
- queries: bfloat16 [16384, 2048], P('ctx', 'exp'), may hold values from -108 to 108
- keys: bfloat16 [16384, 512], P('ctx'), may hold values from -4.5 to 4.5
- values: bfloat16 [16384, 512], P('ctx'), may hold values from -5 to 5
- out_proj: bfloat16 [2048, 2048], P('exp'), may hold values from -0.59765625 to 0.59765625
- norm_gain: bfloat16 [2048], replicated, may hold values from 0.099609375 to 1.8984375
- gate_proj: bfloat16 [128, 2048, 768], P(('ctx', 'exp')), may hold values from -0.125 to 0.125
- up_proj: bfloat16 [128, 2048, 768], P(('ctx', 'exp')), may hold values from -0.125 to 0.125
- down_proj: bfloat16 [128, 768, 2048], P(('ctx', 'exp')), may hold values from -0.21875 to 0.21875
- expert_ids: int32 [16384, 8], P(('ctx', 'exp')), may hold values from 0 to 127, all different within a row; in each aligned block of 128 rows (0 to 127, 128 to 255, ...) at most 9 rows name the same one
- route_weights: float32 [16384, 8], P(('ctx', 'exp')), may hold values from 0.02 to 1
- segment_lengths: int32 [17], replicated, may hold values from 1 to 8192, 16384 in all
Outputs:
- mixed: bfloat16 [16384, 2048], P(('ctx', 'exp'))
The draws below stay inside these ranges and needn't reach their ends.
Inputs may be any that keep to these rules, and one draw needn't show every extreme that they name: `expert_ids`: each position names 8 different experts; among the 128 positions of one device no expert is named more than 9 times, a bound that some block reaches. `segment_lengths`: they sum to 16384.
All inputs are finite; a program needn't handle non-finite values.
Results may differ from the reference program's by a relative error of at most 0.023.
Values may be sent and summed in bfloat16 or wider, within the bound.
No kernel may reach another device: no remote copies, remote signals or barrier semaphores. Data moves between devices by JAX's collectives and lax.ppermute only.
A program may use at most 128 MiB of HBM per device.

```python
import math
import jax
import jax.numpy as jnp
import numpy as np
from jax import lax

D = 2048
HD = 128
KVH = 4
H = 768
TOPK = 8
HQ = 16
RESP = 16
TOK_DEV = 128
SEQ = 16384
E = 128
CAP = 9
N_CTX = 16
N_EXP = 8


def shared_draw(key):
    key_keys = jax.random.fold_in(key, 0)
    base = jnp.clip(jax.random.normal(key_keys, (SEQ, KVH * HD), jnp.float32), -4.5, 4.5)
    return base


def draw_keys(key, part):
    base = shared_draw(key)
    return base.astype(jnp.bfloat16)


def draw_queries(key, part):
    key = jax.random.fold_in(key, 7)
    drawn = jnp.clip(jax.random.normal(key, (SEQ, HQ * HD), jnp.float32), -4.5, 4.5)
    return drawn.astype(jnp.bfloat16)


def draw_stream(key, part):
    key = jax.random.fold_in(key, 11)
    key_row, key_col, key_core = jax.random.split(key, 3)
    row_scale = jnp.exp(jax.random.uniform(key_row, (SEQ, 1), jnp.float32, 0.0, math.log(10.0)))
    col_scale = jnp.exp(jax.random.uniform(key_col, (1, D), jnp.float32, 0.0, math.log(10.0)))
    core = jnp.clip(jax.random.normal(key_core, (SEQ, D), jnp.float32), -4.0, 4.0)
    return (0.01 * row_scale * col_scale * core).astype(jnp.bfloat16)


def block_scale(stream_key, dims, pieces, smallest, largest):
    factor_of = 1.0
    for axis_at, parts in pieces:
        heights = jax.random.uniform(jax.random.fold_in(jax.random.fold_in(stream_key, 6), axis_at), (parts,), jnp.float32, smallest / len(pieces), largest / len(pieces))
        factor_of = factor_of * jnp.repeat(jnp.exp(heights), dims[axis_at] // parts).reshape((-1,) + (1,) * (len(dims) - 1 - axis_at))
    return factor_of


def profile(amount, total, most, lean):
    weights = [(1 << 20) // math.isqrt(standing ** lean) + 1 for standing in range(2, amount + 1)]
    rest, given = total - most - (amount - 1), [1] * (amount - 1)
    while rest > 0:
        free = [i for i in range(amount - 1) if given[i] < most]
        pool, left = sum([weights[i] for i in free]), rest
        for i in free:
            addition = min(most - given[i], max(1, left * weights[i] // pool), rest)
            given[i] = given[i] + addition
            rest = rest - addition
    return np.array([most] + given)


def ragged(rng, number_of, total, reach, skew):
    if number_of == 2:
        one = jax.random.randint(rng, (), max(1, total - reach), min(reach, total - 1) + 1)
        return jnp.stack([one, total - one])
    sizes = jnp.asarray(profile(number_of, total, reach, skew), jnp.int32)
    couples = (number_of - 1) // 2
    source_of, sink = sizes[1:1 + 2 * couples:2], sizes[2:2 + 2 * couples:2]
    margin = jnp.minimum(source_of - 1, reach - sink)
    passed = jax.random.randint(jax.random.fold_in(rng, 1), (couples,), 0, 1 << 20) % (margin + 1)
    sizes = sizes.at[1:1 + 2 * couples:2].set(source_of - passed).at[2:2 + 2 * couples:2].set(sink + passed)
    return sizes[jax.random.permutation(jax.random.fold_in(rng, 2), number_of)]


def shared_out(own_key, own, number, rows, number_of, top, most, slope):
    order = jax.random.permutation(own_key, number_of)
    heavy_load, usual = portions_of(number_of, rows * top, most, slope, True), portions_of(number_of, rows * top, most, slope, False)
    places = jnp.arange(number_of)

    def named(lengths, rotation):
        used = int((lengths > 0).sum())
        fixed = max(1, used // 4)
        passed = fixed + (places - fixed + rotation * (used - fixed)) % max(1, number_of - fixed)
        return jnp.zeros((number_of,), jnp.int32).at[order[jnp.where(places < fixed, places, passed)]].set(jnp.asarray(lengths, jnp.int32))

    lengths = jnp.where(number % 4 == 0, named(heavy_load, number // 4), named(usual, number - number // 4 - 1))
    mixed = jax.random.permutation(jax.random.fold_in(own, 3), number_of)
    source_of, taker = mixed[0:number_of // 2 * 2:2], mixed[1:number_of // 2 * 2:2]
    slack = jnp.minimum(lengths[source_of] - 1, most - lengths[taker]) // 2
    slack = jnp.where((source_of == order[0]) | (taker == order[0]) | (lengths[taker] == 0), 0, jnp.maximum(slack, 0))
    passed = jax.random.randint(jax.random.fold_in(own, 4), (number_of // 2,), 0, 1 << 20) % (slack + 1)
    lengths = lengths.at[source_of].add(-passed).at[taker].add(passed)
    members = jnp.searchsorted(jnp.cumsum(lengths), jnp.arange(rows * top), side="right").astype(jnp.int32)
    grid = members.reshape(top, rows).T
    grid = grid[jax.random.permutation(jax.random.fold_in(own, 1), rows)]
    rotation = jax.random.randint(jax.random.fold_in(own, 2), (rows, 1), 0, top)
    return jnp.take_along_axis(grid, (jnp.arange(top)[None, :] + rotation) % top, axis=1)


def portions_of(number_of, total, reach, skew, full):
    weights = [(1 << 20) // math.isqrt(grade ** skew) + 1 for grade in range(1, number_of + 1)]
    largest = reach if full else min(reach, max(-(-total // number_of), total * weights[0] // sum(weights)))
    least = 1 if total - largest >= number_of - 1 else 0
    counts, spare = [largest] + [least] * (number_of - 1), total - largest - least * (number_of - 1)
    while spare > 0:
        candidates = [i for i in range(1, number_of) if counts[i] < largest] or [i for i in range(1, number_of) if counts[i] < reach]
        mass, remaining = sum([weights[i] for i in candidates]), spare
        for i in candidates:
            addition = min(reach - counts[i], max(1, remaining * weights[i] // mass), spare)
            counts[i] = counts[i] + addition
            spare = spare - addition
    return np.array(counts)


def gaussian(stream_key, dims, deviation, reach, pieces=(), held_as=jnp.bfloat16):
    level = block_scale(stream_key, dims, pieces, -0.22, 0.18) if pieces else 1.0
    drawn = jax.random.normal(stream_key, dims, jnp.float32) * deviation * level
    return jnp.minimum(jnp.maximum(drawn, -reach), reach).astype(held_as)


def setup_inputs(seed: int = 0) -> dict:
    streams_of = jax.random.split(jax.random.key(seed), 13)
    stream = draw_stream(jax.random.fold_in(streams_of[12], 71), 0)
    queries = draw_queries(jax.random.fold_in(streams_of[12], 71), 0)
    keys = draw_keys(jax.random.fold_in(streams_of[12], 71), 0)
    values = gaussian(streams_of[3], (SEQ, KVH * HD), 1.0, 5.0, ((0, 16),))
    out_proj = gaussian(streams_of[4], (HQ * HD, D), 0.1, 0.59765625, ((0, 8),))
    norm_gain = jnp.clip(1.0 + 0.18 * jax.random.normal(streams_of[5], (D,), jnp.float32), 0.099609375, 1.8984375).astype(jnp.bfloat16)
    gate_proj = gaussian(streams_of[6], (E, D, H), D ** -0.5, 0.125, ((0, 128),))
    up_proj = gaussian(streams_of[7], (E, D, H), D ** -0.5, 0.125, ((0, 128),))
    down_proj = gaussian(streams_of[8], (E, H, D), H ** -0.5, 0.21875, ((0, 128),))
    expert_ids_keys = jax.random.split(jax.random.fold_in(streams_of[9], 1), SEQ // TOK_DEV)
    expert_ids_turns = jax.random.permutation(jax.random.fold_in(streams_of[9], 3), SEQ // TOK_DEV)
    expert_ids = jax.vmap(lambda own, number: shared_out(jax.random.fold_in(streams_of[9], 2), own, number, TOK_DEV, E, TOPK, CAP, 2))(expert_ids_keys, expert_ids_turns).reshape((SEQ, TOPK))
    route_weights = jnp.clip(jnp.exp(math.log(1.0) - 3.912023 * jax.random.uniform(streams_of[10], (SEQ, TOPK), jnp.float32) ** block_scale(streams_of[10], (SEQ, TOPK), ((0, 128),), -0.2, 0.2)), 0.02, 1.0)
    segment_lengths = ragged(streams_of[11], RESP + 1, SEQ, SEQ // 2, 2).astype(jnp.int32)
    return dict(stream=stream, queries=queries, keys=keys, values=values, out_proj=out_proj, norm_gain=norm_gain, gate_proj=gate_proj, up_proj=up_proj, down_proj=down_proj, expert_ids=expert_ids, route_weights=route_weights, segment_lengths=segment_lengths)


def segment_of(positions, ends):
    return lax.optimization_barrier(jnp.sum((positions[:, None] >= ends[None, :]).astype(jnp.int32), axis=1)).astype(jnp.int32)

def expert_rows(rows, weight_gate, weight_up, weight_down):
    gate = jnp.dot(rows, weight_gate, preferred_element_type=jnp.float32)
    upper = jnp.dot(rows, weight_up, preferred_element_type=jnp.float32)
    hidden = (jax.nn.silu(gate) * upper).astype(jnp.bfloat16)
    return jnp.dot(hidden, weight_down, preferred_element_type=jnp.float32).astype(jnp.bfloat16)

def reference(stream, queries, keys, values, out_proj, norm_gain, gate_proj, up_proj, down_proj, expert_ids, route_weights, segment_lengths):
    ends = jnp.cumsum(segment_lengths).astype(jnp.int32)
    positions = jnp.arange(SEQ, dtype=jnp.int32)
    segments = segment_of(positions, ends)
    group = HQ // KVH
    scale = 1.0 / math.sqrt(HD)
    key_heads = jnp.repeat(keys.reshape(SEQ, KVH, HD), group, axis=1).astype(jnp.float32)
    value_heads = jnp.repeat(values.reshape(SEQ, KVH, HD), group, axis=1).astype(jnp.float32)
    query_heads = queries.reshape(SEQ, HQ, HD)
    block = math.gcd(SEQ, 256)

    def attend(index):
        start = (index * block).astype(jnp.int32)
        query_block = lax.dynamic_slice_in_dim(query_heads, start, block, 0).astype(jnp.float32)
        query_pos = start + jnp.arange(block, dtype=jnp.int32)
        query_seg = lax.dynamic_slice_in_dim(segments, start, block, 0)
        visible = (positions[None, :] <= query_pos[:, None]) & ((segments[None, :] == 0) | (segments[None, :] == query_seg[:, None]))
        scores = jnp.einsum('qhd,khd->hqk', query_block, key_heads) * scale
        masked = jnp.where(visible[None], scores, -jnp.inf)
        row_max = lax.optimization_barrier(jnp.max(masked, axis=2, keepdims=True))
        weights = jnp.where(visible[None], jnp.exp(scores - row_max), 0.0)
        totals = lax.optimization_barrier(jnp.sum(weights, axis=2))
        rounded = lax.optimization_barrier(weights.astype(jnp.bfloat16)).astype(jnp.float32)
        output = jnp.einsum('hqk,khd->qhd', rounded, value_heads) / jnp.transpose(totals)[:, :, None]
        return output.astype(jnp.bfloat16).reshape(block, HQ * HD)
    attended = lax.map(attend, jnp.arange(SEQ // block, dtype=jnp.int32)).reshape(SEQ, HQ * HD)
    projected = jnp.dot(attended, out_proj, preferred_element_type=jnp.float32)
    residual = stream.astype(jnp.float32) + projected
    normed = (residual * lax.rsqrt(lax.optimization_barrier(jnp.mean(residual * residual, axis=1, keepdims=True)) + 1e-06) * norm_gain.astype(jnp.float32)).astype(jnp.bfloat16)
    shares = route_weights / lax.optimization_barrier(jnp.sum(route_weights, axis=1, keepdims=True))
    most_rows = CAP * N_CTX * N_EXP

    def per_expert(number, carry):
        chosen = expert_ids == number
        selected = jnp.any(chosen, axis=1)
        weight_row = lax.optimization_barrier(jnp.sum(jnp.where(chosen, shares, 0.0), axis=1))
        rows = jnp.nonzero(selected, size=most_rows, fill_value=SEQ)[0].astype(jnp.int32)
        safe_rows = jnp.minimum(rows, SEQ - 1)
        outputs = expert_rows(normed[safe_rows], gate_proj[number], up_proj[number], down_proj[number])
        factor = jnp.where(rows < SEQ, weight_row[safe_rows], 0.0)
        return carry.at[rows].add(factor[:, None] * outputs.astype(jnp.float32), mode='drop')
    routed = lax.fori_loop(0, E, per_expert, jnp.zeros((SEQ, D), jnp.float32))
    return (residual + routed).astype(jnp.bfloat16)
```

```python
import functools, math
import jax
import jax.numpy as jnp
from jax import lax
from jax.experimental import pallas as pl
from jax.experimental.pallas import tpu as pltpu
from jax.sharding import PartitionSpec as P

HD = 128
KVH = 4
HQ = 16
RESP1 = 17

def attend_kernel(TQ, TK, RC, place_ref, lengths_ref, q_ref, kv_ref, out_ref, q_s, m_s, acc_s, v_s):
    rows = q_ref.shape[0]
    M = 2 * TQ
    base = place_ref[0]
    prompt = lengths_ref[0]
    scale = 1.0 / math.sqrt(HD)
    v_s[:, HD:] = jnp.ones((TK, HD), jnp.bfloat16)

    def tile(number, _):
        at = pl.multiple_of(number * TQ, TQ)
        first = base + at
        begin = jnp.int32(0); begin_last = jnp.int32(0); end = jnp.int32(0)
        for s in range(RESP1):
            end = end + lengths_ref[s]
            begin = jnp.where(first >= end, end, begin)
            begin_last = jnp.where(first + TQ - 1 >= end, end, begin_last)
        q_s[:TQ] = q_ref[pl.ds(at, TQ), :HD]
        q_s[TQ:] = q_ref[pl.ds(at, TQ), HD:]
        m_s[...] = jnp.full_like(m_s, -1e30)
        acc_s[...] = jnp.zeros_like(acc_s)
        last = (first + TQ - 1) // TK
        shared = jnp.minimum((prompt + TK - 1) // TK, last + 1)
        own = jnp.maximum(begin // TK, shared)
        count = shared + last + 1 - own

        def block(lo, masked):
            k = kv_ref[pl.ds(lo, TK), :HD]
            v_s[:, :HD] = kv_ref[pl.ds(lo, TK), HD:]
            v = v_s[...]
            for r in range(M // RC):
                rs = pl.ds(r * RC, RC)
                s = lax.dot_general(q_s[rs], k, (((1,), (1,)), ((), ())), preferred_element_type=jnp.float32) * scale
                if masked:
                    pos = first + (r * RC) % TQ + lax.broadcasted_iota(jnp.int32, (min(RC, TQ), 1), 0)
                    starts = jnp.zeros_like(pos)
                    end = jnp.int32(0)
                    for i in range(RESP1):
                        end = end + lengths_ref[i]
                        starts = jnp.where(pos >= end, end, starts)
                    if RC > TQ:
                        pos = jnp.concatenate([pos] * (RC // TQ), axis=0)
                        starts = jnp.concatenate([starts] * (RC // TQ), axis=0)
                    kpos = lo + lax.broadcasted_iota(jnp.int32, (1, TK), 1)
                    seen = (kpos <= pos) & ((kpos < prompt) | (kpos >= starts))
                    s = jnp.where(seen, s, -1e30)
                old = m_s[rs]
                new = jnp.maximum(old, jnp.max(s, axis=1, keepdims=True))
                p = jnp.exp(s - new[:, :1]).astype(jnp.bfloat16)
                pv = jnp.dot(p, v, preferred_element_type=jnp.float32)
                alpha = jnp.exp(old - new)
                acc_s[rs, :HD] = acc_s[rs, :HD] * alpha + pv[:, :HD]
                acc_s[rs, HD:] = acc_s[rs, HD:] * alpha + pv[:, HD:]
                m_s[rs] = new

        def step(i, _):
            j = jnp.where(i < shared, i, own + i - shared)
            lo = pl.multiple_of(j * TK, TK)
            hi = lo + TK
            whole = (hi <= first + 1) & ((hi <= prompt) | (lo >= begin_last))
            pl.when(whole)(lambda: block(lo, False))
            pl.when(jnp.logical_not(whole))(lambda: block(lo, True))
            return 0

        lax.fori_loop(0, count, step, 0)
        o = (acc_s[:, :HD] / acc_s[:, HD:]).astype(jnp.bfloat16)
        out_ref[pl.ds(at, TQ), :HD] = o[:TQ]
        out_ref[pl.ds(at, TQ), HD:] = o[TQ:]
        return 0

    lax.fori_loop(0, rows // TQ, tile, 0)

def attend(place, lengths, q, kv, TQ=512, TK=1024, RC=128):
    return pl.pallas_call(
        functools.partial(attend_kernel, TQ, TK, RC),
        out_shape=jax.ShapeDtypeStruct(q.shape, jnp.bfloat16),
        in_specs=[pl.BlockSpec(memory_space=pltpu.SMEM)]*2 + [pl.BlockSpec(memory_space=pltpu.VMEM)]*2,
        out_specs=pl.BlockSpec(memory_space=pltpu.VMEM),
        scratch_shapes=[pltpu.VMEM((2*TQ, HD), jnp.bfloat16), pltpu.VMEM((2*TQ, HD), jnp.float32),
            pltpu.VMEM((2*TQ, 2*HD), jnp.float32), pltpu.VMEM((TK, 2*HD), jnp.bfloat16)],
        compiler_params=pltpu.CompilerParams(vmem_limit_bytes=48 << 20),
        name="attend",
    )(place, lengths, q, kv)

LANES = 128
VM = pl.BlockSpec(memory_space=pltpu.VMEM)
SM = pl.BlockSpec(memory_space=pltpu.SMEM)

def slots_kernel(capacity, ids_ref, weights_ref, place_ref, shares_ref):
    rows, top = ids_ref.shape
    experts = 128
    ids = ids_ref[...]
    lane = lax.broadcasted_iota(jnp.int32, (rows, experts), 1)
    named = [(ids[:, k : k + 1] == lane).astype(jnp.float32) for k in range(top)]
    chosen = functools.reduce(jnp.add, named).astype(jnp.bfloat16)
    before = (
        lax.broadcasted_iota(jnp.int32, (rows, rows), 1)
        < lax.broadcasted_iota(jnp.int32, (rows, rows), 0)
    ).astype(jnp.bfloat16)
    rank = jnp.dot(before, chosen, preferred_element_type=jnp.float32)
    slot = [jnp.sum(one * rank, axis=1, keepdims=True) for one in named]
    place_ref[...] = ids * capacity + jnp.concatenate(slot, axis=1).astype(jnp.int32)
    weights = weights_ref[...]
    shares_ref[...] = weights / jnp.sum(weights, axis=1, keepdims=True)

def slots(ids, weights, capacity):
    return pl.pallas_call(
        functools.partial(slots_kernel, capacity),
        out_shape=(jax.ShapeDtypeStruct(ids.shape, jnp.int32), jax.ShapeDtypeStruct(weights.shape, jnp.float32)),
        in_specs=[VM, VM], out_specs=(VM, VM), name="slots",
    )(ids, weights)

def pack_kernel(place_ref, projected_ref, stream_ref, gain_ref, residual_ref, out_ref, rows32):
    rows, width = stream_ref.shape
    parts = width // LANES
    residual = stream_ref[...].astype(jnp.float32) + projected_ref[...].astype(jnp.float32)
    spread = lax.rsqrt(jnp.mean(residual * residual, axis=1, keepdims=True) + 1e-06)
    normed = residual * spread * gain_ref[...].astype(jnp.float32)
    for part in range(parts):
        residual_ref[:, part, :] = residual[:, part * LANES : (part + 1) * LANES]
        rows32[:, part, :] = normed[:, part * LANES : (part + 1) * LANES]
    out_ref[...] = jnp.zeros_like(out_ref)

    def one(t, _):
        row = rows32[t].astype(jnp.bfloat16)
        for k in range(8):
            out_ref[place_ref[t * 8 + k]] = row
        return 0
    lax.fori_loop(0, rows, one, 0, unroll=4)

def pack(place, projected, stream, gain, slots_count):
    rows, width = stream.shape
    parts = width // LANES
    return pl.pallas_call(
        pack_kernel,
        out_shape=(jax.ShapeDtypeStruct((rows, parts, LANES), jnp.float32),
                   jax.ShapeDtypeStruct((slots_count, parts, LANES), jnp.bfloat16)),
        in_specs=[SM, VM, VM, VM], out_specs=(VM, VM),
        scratch_shapes=[pltpu.VMEM((rows, parts, LANES), jnp.float32)],
        compiler_params=pltpu.CompilerParams(vmem_limit_bytes=48 << 20),
        name="pack",
    )(place, projected, stream, gain)

TR = 384

def experts_kernel(x_ref, gate_ref, up_ref, down_ref, out_ref, rows32, rows16, back32):
    parts = x_ref.shape[1]
    rows32[...] = x_ref[...].astype(jnp.float32)
    for part in range(parts):
        rows16[:, part * LANES : (part + 1) * LANES] = rows32[:, part, :].astype(jnp.bfloat16)
    rows = rows16[...]
    gate = jnp.dot(rows, gate_ref[0], preferred_element_type=jnp.float32)
    upper = jnp.dot(rows, up_ref[0], preferred_element_type=jnp.float32)
    hidden = (gate / (1.0 + jnp.exp(-gate)) * upper).astype(jnp.bfloat16)
    result = jnp.dot(hidden, down_ref[0], preferred_element_type=jnp.float32)
    for part in range(parts):
        back32[:, part, :] = result[:, part * LANES : (part + 1) * LANES]
    out_ref[...] = back32[...].astype(jnp.bfloat16)

def experts(x, gate, up, down):
    count, parts, lanes = x.shape
    width = parts * lanes
    hidden = gate.shape[2]
    return pl.pallas_call(
        experts_kernel,
        out_shape=jax.ShapeDtypeStruct(x.shape, jnp.bfloat16),
        grid=(count // TR,),
        in_specs=[pl.BlockSpec((TR, parts, lanes), lambda i: (i, 0, 0)),
                  pl.BlockSpec(gate.shape, lambda i: (0, 0, 0)),
                  pl.BlockSpec(up.shape, lambda i: (0, 0, 0)),
                  pl.BlockSpec(down.shape, lambda i: (0, 0, 0))],
        out_specs=pl.BlockSpec((TR, parts, lanes), lambda i: (i, 0, 0)),
        scratch_shapes=[pltpu.VMEM((TR, parts, lanes), jnp.float32), pltpu.VMEM((TR, width), jnp.bfloat16),
                        pltpu.VMEM((TR, parts, lanes), jnp.float32)],
        compiler_params=pltpu.CompilerParams(vmem_limit_bytes=56 << 20),
        name="experts",
    )(x, gate, up, down)

def combine_kernel(place_ref, shares_ref, residual_ref, back_ref, out_ref, total):
    rows, parts, lanes = residual_ref.shape
    def one(t, _):
        acc = residual_ref[t]
        for k in range(8):
            acc = acc + shares_ref[t * 8 + k] * back_ref[place_ref[t * 8 + k]].astype(jnp.float32)
        total[t] = acc
        return 0
    lax.fori_loop(0, rows, one, 0, unroll=2)
    for part in range(parts):
        out_ref[:, part * LANES : (part + 1) * LANES] = total[:, part, :].astype(jnp.bfloat16)

def combine(place, shares, residual, back):
    rows, parts, lanes = residual.shape
    return pl.pallas_call(
        combine_kernel,
        out_shape=jax.ShapeDtypeStruct((rows, parts * lanes), jnp.bfloat16),
        in_specs=[SM, SM, VM, VM], out_specs=VM,
        scratch_shapes=[pltpu.VMEM((rows, parts, lanes), jnp.float32)],
        compiler_params=pltpu.CompilerParams(vmem_limit_bytes=48 << 20),
        name="combine",
    )(place, shares, residual, back)


def on_device(
    stream,
    queries,
    keys,
    values,
    out_proj,
    norm_gain,
    gate_proj,
    up_proj,
    down_proj,
    expert_ids,
    route_weights,
    segment_lengths,
):
    ctx_count = lax.axis_size("ctx")
    exp_count = lax.axis_size("exp")
    ctx_index = lax.axis_index("ctx")
    exp_index = lax.axis_index("exp")
    rows_ctx = queries.shape[0]
    heads_here = queries.shape[1] // HD
    group = HQ // KVH
    expert_count = ctx_count * exp_count
    tok_rows, top_count = expert_ids.shape
    capacity = max(2, tok_rows * top_count * 9 // (expert_count * 8))
    kv_start = exp_index * heads_here // group * HD
    own = jnp.concatenate(
        [
            lax.dynamic_slice_in_dim(keys, kv_start, HD, 1),
            lax.dynamic_slice_in_dim(values, kv_start, HD, 1),
        ],
        axis=1,
    )
    place, shares = slots(expert_ids, route_weights, capacity)
    place = place.reshape(-1)
    shares = shares.reshape(-1)
    gathered = lax.all_gather(own, "ctx", axis=0, tiled=True)
    first = (ctx_index * rows_ctx).astype(jnp.int32).reshape(1)
    attended = attend(first, segment_lengths, queries, gathered)
    projected = lax.psum_scatter(
        jnp.dot(attended, out_proj, preferred_element_type=jnp.float32).astype(jnp.bfloat16),
        "exp",
        scatter_dimension=0,
        tiled=True,
    )
    residual, outgoing = pack(
        place, projected, stream, norm_gain.reshape(1, -1), expert_count * capacity
    )
    shape = (expert_count, capacity) + outgoing.shape[1:]
    arrived = lax.all_to_all(
        outgoing.reshape(shape), ("ctx", "exp"), split_axis=0, concat_axis=0, tiled=True
    )
    results = experts(arrived.reshape(outgoing.shape), gate_proj, up_proj, down_proj)
    returned = lax.all_to_all(
        results.reshape(shape), ("ctx", "exp"), split_axis=0, concat_axis=0, tiled=True
    )
    return combine(place, shares, residual, returned.reshape(outgoing.shape))


def solution(mesh):
    placed = (
        P(("ctx", "exp"), None),
        P("ctx", "exp"),
        P("ctx", None),
        P("ctx", None),
        P("exp", None),
        P(),
        P(("ctx", "exp"), None, None),
        P(("ctx", "exp"), None, None),
        P(("ctx", "exp"), None, None),
        P(("ctx", "exp"), None),
        P(("ctx", "exp"), None),
        P(),
    )
    return jax.shard_map(
        on_device, mesh=mesh, in_specs=placed, out_specs=P(("ctx", "exp"), None), check_vma=False
    )
```

```python
import functools
import math

import jax
import jax.numpy as jnp
from jax import lax
from jax.experimental import pallas as pl
from jax.experimental.pallas import tpu as pltpu
from jax.sharding import PartitionSpec as P

HD = 128
KVH = 4
HQ = 16
LANES = 128
SEGMENTS = 17
SHARD = 1024
HALF = 8
TQ = 1024
RC = 256
NEVER = -1e30
VM = pl.BlockSpec(memory_space=pltpu.VMEM)
SM = pl.BlockSpec(memory_space=pltpu.SMEM)
HBM = pl.BlockSpec(memory_space=pl.ANY)


def attend_part(final, meta_ref, lengths_ref, *refs):
    pieces = refs[:10]
    if final:
        q_ref, out_ref, lse_ref, kv_s, q_s, m_s, acc_s, v_s, sems = refs[10:]
    else:
        q_refs, out_refs = refs[10:12], refs[12:14]
        kv_s, q_s, m_s, acc_s, v_s, sems = refs[14:]
    base, low, active, z, core = (meta_ref[i] for i in range(5))
    prompt = lengths_ref[0]
    scale = math.log2(math.e) / math.sqrt(HD)

    first = base
    begin = jnp.int32(0)
    begin_last = jnp.int32(0)
    end = jnp.int32(0)
    for s in range(SEGMENTS):
        end = end + lengths_ref[s]
        begin = jnp.where(first >= end, end, begin)
        begin_last = jnp.where(first + TQ - 1 >= end, end, begin_last)
    last = (first + TQ - 1) // SHARD
    shared = jnp.minimum((prompt + SHARD - 1) // SHARD, last + 1)
    own = jnp.maximum(begin // SHARD, shared)
    one_from, one_to = low, jnp.minimum(shared, low + HALF)
    two_from, two_to = jnp.maximum(own, low), jnp.minimum(last + 1, low + HALF)
    one_count = jnp.maximum(one_to - one_from, 0)
    count = one_count + jnp.maximum(two_to - two_from, 0)

    copies = []
    for other in range(2):
        side = core if other == 0 else 1 - core
        for n, (dz, begin_row) in enumerate(((0, 0), (3, 0), (1, 0), (2, 0), (2, SHARD // 2))):
            piece = pieces[other * 5 + n]
            shard = ((z + dz) & 3) * 2 + side
            target = kv_s.at[shard, pl.ds(begin_row, piece.shape[0])]
            number = low + shard
            used = (number < one_to) | ((number >= two_from) & (number < two_to))
            copies.append(
                ((active > 0) & used, pltpu.make_async_copy(piece, target, sems.at[other * 5 + n]))
            )

    for used, copy in copies:
        pl.when(used)(copy.start)

    @pl.when(active > 0)
    def _():
        v_s[:, HD:] = jnp.ones((SHARD, HD), jnp.bfloat16)
        for head in range(2):
            hs = slice(head * HD, (head + 1) * HD)
            if final:
                q = q_ref[:, hs].astype(jnp.float32) * scale
            else:
                q = jnp.concatenate([ref[:, hs] for ref in q_refs], axis=0).astype(jnp.float32) * scale
            rounded = q.astype(jnp.bfloat16)
            q_s[head * TQ : (head + 1) * TQ, :HD] = rounded
            q_s[head * TQ : (head + 1) * TQ, HD:] = (q - rounded.astype(jnp.float32)).astype(jnp.bfloat16)
        m_s[...] = jnp.full_like(m_s, NEVER)
        acc_s[...] = jnp.zeros_like(acc_s)

    for used, copy in copies:
        pl.when(used)(copy.wait)

    @pl.when(active > 0)
    def _():
        def block(number, masked):
            lo = number * SHARD
            k = kv_s[number - low, :, :HD]
            k = jnp.concatenate([k, k], axis=1)
            v_s[:, :HD] = kv_s[number - low, :, HD:]
            v = v_s[...]

            def score(r):
                return lax.dot_general(
                    q_s[pl.ds(r * RC, RC)], k, (((1,), (1,)), ((), ())), preferred_element_type=jnp.float32
                )

            ahead = score(0)
            for r in range(2 * TQ // RC):
                rs = pl.ds(r * RC, RC)
                s = ahead
                if r + 1 < 2 * TQ // RC:
                    ahead = score(r + 1)
                if masked:
                    pos = first + (r * RC) % TQ + lax.broadcasted_iota(jnp.int32, (RC, 1), 0)
                    starts = jnp.zeros_like(pos)
                    end = jnp.int32(0)
                    for i in range(SEGMENTS):
                        end = end + lengths_ref[i]
                        starts = jnp.where(pos >= end, end, starts)
                    kpos = lo + lax.broadcasted_iota(jnp.int32, (1, SHARD), 1)
                    seen = jnp.where(kpos < prompt, SHARD * 2 * HALF, kpos) >= starts
                    if final:
                        seen = seen & (kpos <= pos)
                    s = jnp.where(seen, s, NEVER)
                old = m_s[rs]
                new = jnp.maximum(old, jnp.max(s, axis=1, keepdims=True))
                p = jnp.exp2(s - new[:, :1]).astype(jnp.bfloat16)
                m_s[rs] = new
                alpha = jnp.exp2(old - new)
                pv = jnp.dot(p, v, preferred_element_type=jnp.float32)
                acc_s[rs, :HD] = acc_s[rs, :HD] * alpha + pv[:, :HD]
                acc_s[rs, HD:] = acc_s[rs, HD:] * alpha + pv[:, HD:]

        def step(i, _):
            number = jnp.where(i < one_count, one_from + i, two_from + i - one_count)
            lo = number * SHARD
            hi = lo + SHARD
            whole = (hi <= first + 1) & ((hi <= prompt) | (lo >= begin_last))
            pl.when(whole)(lambda: block(number, False))
            pl.when(jnp.logical_not(whole))(lambda: block(number, True))
            return 0

        lax.fori_loop(0, count, step, 0)
        for head in range(2):
            hs = pl.ds(head * TQ, TQ)
            total = acc_s[hs, HD:]
            o = acc_s[hs, :HD] / total
            lse = m_s[hs] + jnp.log2(total)
            if final:
                out_ref[:, head * HD : (head + 1) * HD] = o
                lse_ref[:, head * HD : (head + 1) * HD] = lse
            else:
                a = lse.astype(jnp.bfloat16).astype(jnp.float32)
                b = (lse - a).astype(jnp.bfloat16).astype(jnp.float32)
                c = lse - a - b
                lane = lax.broadcasted_iota(jnp.int32, (TQ, LANES), 1)
                parts = jnp.where(lane == 0, a, jnp.where(lane == 1, b, c)).astype(jnp.bfloat16)
                o = o.astype(jnp.bfloat16)
                half = TQ // 2
                for n in range(2):
                    out_refs[n][:, head * HD : (head + 1) * HD] = o[n * half : (n + 1) * half]
                    out_refs[n][:, (2 + head) * HD : (3 + head) * HD] = parts[n * half : (n + 1) * half]


def attend(final, meta, lengths, q, pieces, blocks):
    if final:
        shapes = tuple(jax.ShapeDtypeStruct((SHARD, 2 * HD), jnp.float32) for _ in range(2))
    else:
        shapes = tuple(jax.ShapeDtypeStruct((TQ // 2, 4 * HD), jnp.bfloat16) for _ in range(2))
    return pl.pallas_call(
        functools.partial(attend_part, final),
        out_shape=shapes,
        in_specs=[SM, SM] + [HBM] * 10 + [VM] * len(q),
        out_specs=(VM, VM),
        scratch_shapes=[
            pltpu.VMEM((HALF, SHARD, 2 * HD), jnp.bfloat16),
            pltpu.VMEM((2 * TQ, 2 * HD), jnp.bfloat16),
            pltpu.VMEM((2 * TQ, HD), jnp.float32),
            pltpu.VMEM((2 * TQ, 2 * HD), jnp.float32),
            pltpu.VMEM((SHARD, 2 * HD), jnp.bfloat16),
            pltpu.SemaphoreType.DMA((10,)),
        ],
        compiler_params=pltpu.CompilerParams(vmem_limit_bytes=60 << 20),
        cost_estimate=pl.CostEstimate(
            flops=blocks * 32 * HD * SHARD * SHARD, bytes_accessed=8 << 20, transcendentals=blocks * 2 * SHARD * SHARD
        ),
        name="attend_own" if final else "attend_sent",
    )(meta, lengths, *pieces, *q)


def merge_kernel(meta_ref, first_ref, second_ref, own_ref, lse_ref, out_ref):
    high = meta_ref[0] > 0
    half = first_ref.shape[0]
    for n, sent_ref in enumerate((first_ref, second_ref)):
        rs = pl.ds(n * half, half)
        for head in range(2):
            hs = pl.ds(head * HD, HD)
            parts = sent_ref[:, (2 + head) * HD : (3 + head) * HD].astype(jnp.float32)
            sent = parts[:, 0:1] + parts[:, 1:2] + parts[:, 2:3]
            sent = jnp.where(high, sent, NEVER)
            here = lse_ref[rs, hs]
            top = jnp.maximum(sent, here)
            w_sent = jnp.exp2(sent - top)
            w_here = jnp.exp2(here - top)
            o = w_sent * sent_ref[:, hs].astype(jnp.float32) + w_here * own_ref[rs, hs]
            out_ref[rs, hs] = (o / (w_sent + w_here)).astype(jnp.bfloat16)


def merge(meta, first, second, own, lse):
    return pl.pallas_call(
        merge_kernel,
        out_shape=jax.ShapeDtypeStruct(own.shape, jnp.bfloat16),
        in_specs=[SM, VM, VM, VM, VM],
        out_specs=VM,
        compiler_params=pltpu.CompilerParams(vmem_limit_bytes=32 << 20),
        name="merge",
    )(meta, first, second, own, lse)


def slots_kernel(capacity, ids_ref, weights_ref, place_ref, shares_ref):
    rows, top = ids_ref.shape
    experts = 128
    ids = ids_ref[...]
    lane = lax.broadcasted_iota(jnp.int32, (rows, experts), 1)
    named = [(ids[:, k : k + 1] == lane).astype(jnp.float32) for k in range(top)]
    chosen = functools.reduce(jnp.add, named).astype(jnp.bfloat16)
    before = (
        lax.broadcasted_iota(jnp.int32, (rows, rows), 1)
        < lax.broadcasted_iota(jnp.int32, (rows, rows), 0)
    ).astype(jnp.bfloat16)
    rank = jnp.dot(before, chosen, preferred_element_type=jnp.float32)
    slot = [jnp.sum(one * rank, axis=1, keepdims=True) for one in named]
    place_ref[...] = ids * capacity + jnp.concatenate(slot, axis=1).astype(jnp.int32)
    weights = weights_ref[...]
    shares_ref[...] = weights / jnp.sum(weights, axis=1, keepdims=True)

def slots(ids, weights, capacity):
    return pl.pallas_call(
        functools.partial(slots_kernel, capacity),
        out_shape=(jax.ShapeDtypeStruct(ids.shape, jnp.int32), jax.ShapeDtypeStruct(weights.shape, jnp.float32)),
        in_specs=[VM, VM], out_specs=(VM, VM), name="slots",
    )(ids, weights)

def pack_kernel(
    meta_ref, place_ref, attended_ref, near_ref, far_ref, stream_ref, gain_ref, residual_ref, out_ref, rows32
):
    rows, width = stream_ref.shape
    parts = width // LANES
    upper = meta_ref[0] > 0
    near, far = [], []
    for e in range(attended_ref.shape[0]):
        a, b = attended_ref[e, :, :LANES], attended_ref[e, :, LANES:]
        near.append(jnp.where(upper, b, a))
        far.append(jnp.where(upper, a, b))
    projected = jnp.dot(
        jnp.concatenate(near, axis=1), near_ref[...], preferred_element_type=jnp.float32
    ) + jnp.dot(jnp.concatenate(far, axis=1), far_ref[...], preferred_element_type=jnp.float32)
    residual = stream_ref[...].astype(jnp.float32) + projected
    spread = lax.rsqrt(jnp.mean(residual * residual, axis=1, keepdims=True) + 1e-06)
    normed = residual * spread * gain_ref[...].astype(jnp.float32)
    residual_ref[...] = residual.reshape(rows, parts, LANES)
    rows32[...] = normed.astype(jnp.bfloat16).reshape(rows, parts, LANES)
    out_ref[...] = jnp.zeros_like(out_ref)

    def one(t, _):
        row = rows32[t]
        for k in range(8):
            out_ref[place_ref[t * 8 + k]] = row
        return 0
    lax.fori_loop(0, rows, one, 0, unroll=4)

def pack(meta, place, attended, near, far, stream, gain, slots_count):
    rows, width = stream.shape
    parts = width // LANES
    return pl.pallas_call(
        pack_kernel,
        out_shape=(
            jax.ShapeDtypeStruct((rows, parts, LANES), jnp.float32),
            jax.ShapeDtypeStruct((slots_count, parts, LANES), jnp.bfloat16),
        ),
        in_specs=[SM, SM] + [VM] * 5,
        out_specs=(VM, VM),
        scratch_shapes=[pltpu.VMEM((rows, parts, LANES), jnp.bfloat16)],
        compiler_params=pltpu.CompilerParams(vmem_limit_bytes=32 << 20),
        name="pack",
    )(meta, place, attended, near, far, stream, gain)


TR = 384


def experts_kernel(x_ref, gate_ref, up_ref, down_ref, out_ref):
    rows, parts, lanes = x_ref.shape
    x = x_ref[...].reshape(rows, parts * lanes)
    gate = jnp.dot(x, gate_ref[0], preferred_element_type=jnp.float32)
    upper = jnp.dot(x, up_ref[0], preferred_element_type=jnp.float32)
    hidden = (gate / (1.0 + jnp.exp(-gate)) * upper).astype(jnp.bfloat16)
    result = jnp.dot(hidden, down_ref[0], preferred_element_type=jnp.float32)
    out_ref[...] = result.astype(jnp.bfloat16).reshape(rows, parts, lanes)


def experts(x, gate, up, down):
    count, parts, lanes = x.shape
    return pl.pallas_call(
        experts_kernel,
        out_shape=jax.ShapeDtypeStruct(x.shape, jnp.bfloat16),
        grid=(count // TR,),
        in_specs=[
            pl.BlockSpec((TR, parts, lanes), lambda i: (i, 0, 0)),
            VM,
            VM,
            VM,
        ],
        out_specs=pl.BlockSpec((TR, parts, lanes), lambda i: (i, 0, 0)),
        compiler_params=pltpu.CompilerParams(vmem_limit_bytes=36 << 20),
        name="experts",
    )(x, gate, up, down)


def combine_kernel(place_ref, shares_ref, residual_ref, back_ref, out_ref, total):
    rows, parts, lanes = residual_ref.shape
    def one(t, _):
        acc = residual_ref[t]
        for k in range(8):
            acc = acc + shares_ref[t * 8 + k] * back_ref[place_ref[t * 8 + k]].astype(jnp.float32)
        total[t] = acc.astype(jnp.bfloat16)
        return 0
    lax.fori_loop(0, rows, one, 0, unroll=2)
    out_ref[...] = total[...].reshape(rows, parts * lanes)

def combine(place, shares, residual, back):
    rows, parts, lanes = residual.shape
    return pl.pallas_call(
        combine_kernel,
        out_shape=jax.ShapeDtypeStruct((rows, parts * lanes), jnp.bfloat16),
        in_specs=[SM, SM, VM, VM], out_specs=VM,
        scratch_shapes=[pltpu.VMEM((rows, parts, lanes), jnp.bfloat16)],
        compiler_params=pltpu.CompilerParams(vmem_limit_bytes=48 << 20),
        name="combine",
    )(place, shares, residual, back)


def permute(x, move):
    pairs = []
    for n in range(128):
        ctx, exp = divmod(n, 8)
        x_lo, z, core = ctx // 8, ctx // 2 % 4, ctx % 2
        y, x_hi = exp // 2, exp % 2
        target = move(x_hi * 2 + x_lo, y, z, core)
        if target is None:
            continue
        tx, ty, tz, tc = target
        tx, ty, tz = tx % 4, ty % 4, tz % 4
        pairs.append((n, ((tx % 2) * 8 + tz * 2 + tc) * 8 + ty * 2 + tx // 2))
    return lax.ppermute(x, ("ctx", "exp"), pairs)


def along_z(a, step):
    return permute(a, lambda x, y, z, c: (x, y, z + step, c))


def along_y(a, step):
    return permute(a, lambda x, y, z, c: (x, y + step, z, c))


def other_core(a):
    return permute(a, lambda x, y, z, c: (x, y, z, 1 - c))


def down_x(a, step):
    return permute(a, lambda x, y, z, c: (x + step, y, z, c) if x % 2 == 1 else None)


def back_x(a, step):
    return permute(a, lambda x, y, z, c: (x + step, y, z, c) if x % 2 == 0 else None)


def on_device(
    stream,
    queries,
    keys,
    values,
    out_proj,
    norm_gain,
    gate_proj,
    up_proj,
    down_proj,
    expert_ids,
    route_weights,
    segment_lengths,
):
    ctx_count = lax.axis_size("ctx")
    exp_count = lax.axis_size("exp")
    ctx_index = lax.axis_index("ctx").astype(jnp.int32)
    exp_index = lax.axis_index("exp").astype(jnp.int32)
    rows_ctx = queries.shape[0]
    expert_count = ctx_count * exp_count
    tok_rows, top_count = expert_ids.shape
    capacity = max(2, tok_rows * top_count * 9 // (expert_count * 8))
    x_lo, z, core = ctx_index // 8, ctx_index // 2 % 4, ctx_index % 2
    y = exp_index // 2
    own = jnp.concatenate(
        [lax.dynamic_slice_in_dim(keys, y * HD, HD, 1), lax.dynamic_slice_in_dim(values, y * HD, HD, 1)],
        axis=1,
    )
    middle = rows_ctx // 2
    up, down = along_z(own, 1), along_z(own, -1)
    q_sent = (down_x(queries[:middle], -1), down_x(queries[middle:], 1))
    far_a, far_b = along_z(up[:middle], 1), along_z(down[middle:], -1)
    near = (own, up, down, far_a, far_b)
    pieces = near + tuple(other_core(piece) for piece in near)

    mine = lax.dynamic_slice_in_dim(out_proj, core * LANES, LANES, 0)
    w_near = lax.all_gather(mine, "exp", axis=0, tiled=True)

    place, shares = slots(expert_ids, route_weights, capacity)
    place = place.reshape(-1)
    shares = shares.reshape(-1)

    low = x_lo * HALF
    one = jnp.int32(1)
    meta_sent = jnp.stack([(ctx_index + HALF) * rows_ctx, low, one - x_lo, z, core])
    meta_own = jnp.stack([ctx_index * rows_ctx, low, one, z, core])
    sent = attend(False, meta_sent, segment_lengths, q_sent, pieces, 4)
    meta_own, first, second = lax.optimization_barrier((meta_own, *sent))
    first, second = back_x(first, 1), back_x(second, -1)
    partial, lse = attend(True, meta_own, segment_lengths, (queries,), pieces, 5)
    attended = merge(x_lo.reshape(1), first, second, partial, lse)
    w_near, attended = lax.optimization_barrier((w_near, attended))
    w_far = other_core(w_near)
    spread = lax.all_to_all(
        attended.reshape(exp_count, tok_rows, 2 * HD), "exp", split_axis=0, concat_axis=0, tiled=True
    )
    residual, outgoing = pack(
        core.reshape(1),
        place,
        spread,
        w_near,
        w_far,
        stream,
        norm_gain.reshape(1, -1),
        expert_count * capacity,
    )
    shape = (expert_count, capacity) + outgoing.shape[1:]
    arrived = lax.all_to_all(
        outgoing.reshape(shape), ("ctx", "exp"), split_axis=0, concat_axis=0, tiled=True
    )
    results = experts(arrived.reshape(outgoing.shape), gate_proj, up_proj, down_proj)
    returned = lax.all_to_all(
        results.reshape(shape), ("ctx", "exp"), split_axis=0, concat_axis=0, tiled=True
    )
    return combine(place, shares, residual, returned.reshape(outgoing.shape))


def solution(mesh):
    placed = (
        P(("ctx", "exp"), None),
        P("ctx", "exp"),
        P("ctx", None),
        P("ctx", None),
        P("exp", None),
        P(),
        P(("ctx", "exp"), None, None),
        P(("ctx", "exp"), None, None),
        P(("ctx", "exp"), None, None),
        P(("ctx", "exp"), None),
        P(("ctx", "exp"), None),
        P(),
    )
    return jax.shard_map(
        on_device, mesh=mesh, in_specs=placed, out_specs=P(("ctx", "exp"), None), check_vma=False
    )
```

```python
import functools
import math

import jax
import jax.numpy as jnp
from jax import lax
from jax.experimental import pallas as pl
from jax.experimental.pallas import tpu as pltpu
from jax.sharding import PartitionSpec as P

HD = 128
KVH = 4
HQ = 16
LANES = 128
SEGMENTS = 17
SHARD = 1024
HALF = 8
TQ = 1024
RC = 256
NEVER = -1e30
VM = pl.BlockSpec(memory_space=pltpu.VMEM)
SM = pl.BlockSpec(memory_space=pltpu.SMEM)
HBM = pl.BlockSpec(memory_space=pl.ANY)


def attend_part(final, meta_ref, lengths_ref, *refs):
    pieces = refs[:10]
    count_q = 1 if final else 2
    q_refs, out_refs = refs[10 : 10 + count_q], refs[10 + count_q : 12 + count_q]
    kv_s, q_s, m_s, acc_s, v_s, start_s, sems = refs[12 + count_q :]
    ctx = meta_ref[0]
    half, z, core = ctx // HALF, (ctx // 2) & 3, ctx & 1
    low = half * HALF
    if final:
        base, active = ctx * SHARD, jnp.int32(1)
    else:
        base, active = (ctx + HALF) * SHARD, 1 - half
    prompt = lengths_ref[0]
    scale = math.log2(math.e) / math.sqrt(HD)

    first = base
    begin = jnp.int32(0)
    begin_last = jnp.int32(0)
    end = jnp.int32(0)
    for s in range(SEGMENTS):
        end = end + lengths_ref[s]
        begin = jnp.where(first >= end, end, begin)
        begin_last = jnp.where(first + TQ - 1 >= end, end, begin_last)
    last = (first + TQ - 1) // SHARD
    shared = jnp.minimum((prompt + SHARD - 1) // SHARD, last + 1)
    own = jnp.maximum(begin // SHARD, shared)
    one_from, one_to = low, jnp.minimum(shared, low + HALF)
    two_from, two_to = jnp.maximum(own, low), jnp.minimum(last + 1, low + HALF)
    one_count = jnp.maximum(one_to - one_from, 0)
    count = one_count + jnp.maximum(two_to - two_from, 0)

    copies = []
    for other in range(2):
        side = core if other == 0 else 1 - core
        for n, (dz, begin_row) in enumerate(((0, 0), (3, 0), (1, 0), (2, 0), (2, SHARD // 2))):
            piece = pieces[other * 5 + n]
            shard = ((z + dz) & 3) * 2 + side
            target = kv_s.at[shard, pl.ds(begin_row, piece.shape[0])]
            number = low + shard
            used = (number < one_to) | ((number >= two_from) & (number < two_to))
            copies.append(
                ((active > 0) & used, pltpu.make_async_copy(piece, target, sems.at[other * 5 + n]))
            )

    for used, copy in copies:
        pl.when(used)(copy.start)

    @pl.when(active > 0)
    def _():
        v_s[:, HD:] = jnp.ones((SHARD, HD), jnp.bfloat16)
        pos = first + lax.broadcasted_iota(jnp.int32, (TQ, LANES), 0)
        starts = jnp.zeros_like(pos)
        end = jnp.int32(0)
        for i in range(SEGMENTS):
            end = end + lengths_ref[i]
            starts = jnp.where(pos >= end, end, starts)
        start_s[...] = starts
        for head in range(2):
            hs = slice(head * HD, (head + 1) * HD)
            q = jnp.concatenate([ref[:, hs] for ref in q_refs], axis=0).astype(jnp.float32) * scale
            rounded = q.astype(jnp.bfloat16)
            q_s[head * TQ : (head + 1) * TQ, :HD] = rounded
            q_s[head * TQ : (head + 1) * TQ, HD:] = (q - rounded.astype(jnp.float32)).astype(jnp.bfloat16)
        m_s[...] = jnp.full_like(m_s, NEVER)
        acc_s[...] = jnp.zeros_like(acc_s)

    for used, copy in copies:
        pl.when(used)(copy.wait)

    @pl.when(active > 0)
    def _():
        def block(number, masked):
            lo = number * SHARD
            k = kv_s[number - low, :, :HD]
            k = jnp.concatenate([k, k], axis=1)
            v_s[:, :HD] = kv_s[number - low, :, HD:]
            v = v_s[...]

            def score(r):
                return lax.dot_general(
                    q_s[pl.ds(r * RC, RC)], k, (((1,), (1,)), ((), ())), preferred_element_type=jnp.float32
                )

            ahead = score(0)
            for r in range(2 * TQ // RC):
                rs = pl.ds(r * RC, RC)
                s = ahead
                if r + 1 < 2 * TQ // RC:
                    ahead = score(r + 1)
                if masked:
                    pos = first + (r * RC) % TQ + lax.broadcasted_iota(jnp.int32, (RC, 1), 0)
                    starts = start_s[pl.ds((r * RC) % TQ, RC)][:, :1]
                    kpos = lo + lax.broadcasted_iota(jnp.int32, (1, SHARD), 1)
                    seen = jnp.where(kpos < prompt, SHARD * 2 * HALF, kpos) >= starts
                    if final:
                        seen = seen & (kpos <= pos)
                    s = jnp.where(seen, s, NEVER)
                old = m_s[rs]
                new = jnp.maximum(old, jnp.max(s, axis=1, keepdims=True))
                p = jnp.exp2(s - new[:, :1]).astype(jnp.bfloat16)
                m_s[rs] = new
                alpha = jnp.exp2(old - new)
                pv = jnp.dot(p, v, preferred_element_type=jnp.float32)
                acc_s[rs, :HD] = acc_s[rs, :HD] * alpha + pv[:, :HD]
                acc_s[rs, HD:] = acc_s[rs, HD:] * alpha + pv[:, HD:]

        def step(i, _):
            number = jnp.where(i < one_count, one_from + i, two_from + i - one_count)
            lo = number * SHARD
            hi = lo + SHARD
            whole = (hi <= first + 1) & ((hi <= prompt) | (lo >= begin_last))
            pl.when(whole)(lambda: block(number, False))
            pl.when(jnp.logical_not(whole))(lambda: block(number, True))
            return 0

        lax.fori_loop(0, count, step, 0)
        for head in range(2):
            hs = pl.ds(head * TQ, TQ)
            total = acc_s[hs, HD:]
            o = acc_s[hs, :HD] / total
            lse = m_s[hs] + jnp.log2(total)
            a = lse.astype(jnp.bfloat16).astype(jnp.float32)
            b = (lse - a).astype(jnp.bfloat16).astype(jnp.float32)
            c = lse - a - b
            lane = lax.broadcasted_iota(jnp.int32, (TQ, LANES), 1)
            parts = jnp.where(lane == 0, a, jnp.where(lane == 1, b, c)).astype(jnp.bfloat16)
            o = o.astype(jnp.bfloat16)
            rows = TQ // 2
            for n in range(2):
                out_refs[n][:, head * HD : (head + 1) * HD] = o[n * rows : (n + 1) * rows]
                out_refs[n][:, (2 + head) * HD : (3 + head) * HD] = parts[n * rows : (n + 1) * rows]


def attend(final, meta, lengths, q, pieces, blocks):
    shapes = tuple(jax.ShapeDtypeStruct((TQ // 2, 4 * HD), jnp.bfloat16) for _ in range(2))
    return pl.pallas_call(
        functools.partial(attend_part, final),
        out_shape=shapes,
        in_specs=[SM, SM] + [HBM] * 10 + [VM] * len(q),
        out_specs=(VM, VM),
        scratch_shapes=[
            pltpu.VMEM((HALF, SHARD, 2 * HD), jnp.bfloat16),
            pltpu.VMEM((2 * TQ, 2 * HD), jnp.bfloat16),
            pltpu.VMEM((2 * TQ, HD), jnp.float32),
            pltpu.VMEM((2 * TQ, 2 * HD), jnp.float32),
            pltpu.VMEM((SHARD, 2 * HD), jnp.bfloat16),
            pltpu.VMEM((TQ, LANES), jnp.int32),
            pltpu.SemaphoreType.DMA((10,)),
        ],
        compiler_params=pltpu.CompilerParams(vmem_limit_bytes=60 << 20),
        cost_estimate=pl.CostEstimate(
            flops=blocks * 32 * HD * SHARD * SHARD, bytes_accessed=8 << 20, transcendentals=blocks * 2 * SHARD * SHARD
        ),
        name="attend_own" if final else "attend_sent",
    )(meta, lengths, *pieces, *q)


def merge_kernel(meta_ref, *refs):
    sent_refs, own_refs, out_ref = refs[:2], refs[2:4], refs[4]
    high = meta_ref[0] >= HALF
    half = out_ref.shape[0] // 2
    for n in range(2):
        sent_ref, own_ref = sent_refs[n], own_refs[n]
        for head in range(2):
            hs = slice(head * HD, (head + 1) * HD)

            def log_sum(ref):
                parts = ref[:, (2 + head) * HD : (3 + head) * HD].astype(jnp.float32)
                return parts[:, 0:1] + parts[:, 1:2] + parts[:, 2:3]

            sent, here = jnp.where(high, log_sum(sent_ref), NEVER), log_sum(own_ref)
            top = jnp.maximum(sent, here)
            w_sent, w_here = jnp.exp2(sent - top), jnp.exp2(here - top)
            share = w_sent / (w_sent + w_here)
            a, b = sent_ref[:, hs].astype(jnp.float32), own_ref[:, hs].astype(jnp.float32)
            o = share * a + (1.0 - share) * b
            out_ref[n * half : (n + 1) * half, hs] = o.astype(jnp.bfloat16)


def merge(meta, sent, own):
    half = own[0].shape[0]
    return pl.pallas_call(
        merge_kernel,
        out_shape=jax.ShapeDtypeStruct((2 * half, 2 * HD), jnp.bfloat16),
        in_specs=[SM] + [VM] * 4,
        out_specs=VM,
        compiler_params=pltpu.CompilerParams(vmem_limit_bytes=16 << 20),
        name="merge",
    )(meta, *sent, *own)


def slots_kernel(capacity, ids_ref, weights_ref, place_ref, shares_ref):
    rows, top = ids_ref.shape
    experts = 128
    ids = ids_ref[...]
    lane = lax.broadcasted_iota(jnp.int32, (rows, experts), 1)
    named = [(ids[:, k : k + 1] == lane).astype(jnp.float32) for k in range(top)]
    chosen = functools.reduce(jnp.add, named).astype(jnp.bfloat16)
    before = (
        lax.broadcasted_iota(jnp.int32, (rows, rows), 1)
        < lax.broadcasted_iota(jnp.int32, (rows, rows), 0)
    ).astype(jnp.bfloat16)
    rank = jnp.dot(before, chosen, preferred_element_type=jnp.float32)
    slot = [jnp.sum(one * rank, axis=1, keepdims=True) for one in named]
    place_ref[...] = ids * capacity + jnp.concatenate(slot, axis=1).astype(jnp.int32)
    weights = weights_ref[...]
    shares_ref[...] = weights / jnp.sum(weights, axis=1, keepdims=True)

def slots(ids, weights, capacity):
    return pl.pallas_call(
        functools.partial(slots_kernel, capacity),
        out_shape=(jax.ShapeDtypeStruct(ids.shape, jnp.int32), jax.ShapeDtypeStruct(weights.shape, jnp.float32)),
        in_specs=[VM, VM], out_specs=(VM, VM), name="slots",
    )(ids, weights)

def pack_kernel(
    meta_ref, place_ref, attended_ref, near_ref, far_ref, stream_ref, gain_ref, residual_ref, out_ref, rows32
):
    rows, width = stream_ref.shape
    parts = width // LANES
    upper = (meta_ref[0] & 1) > 0
    near, far = [], []
    for e in range(attended_ref.shape[0]):
        a, b = attended_ref[e, :, :LANES], attended_ref[e, :, LANES:]
        near.append(jnp.where(upper, b, a))
        far.append(jnp.where(upper, a, b))
    projected = jnp.dot(
        jnp.concatenate(near, axis=1), near_ref[...], preferred_element_type=jnp.float32
    ) + jnp.dot(jnp.concatenate(far, axis=1), far_ref[...], preferred_element_type=jnp.float32)
    residual = stream_ref[...].astype(jnp.float32) + projected
    spread = lax.rsqrt(jnp.mean(residual * residual, axis=1, keepdims=True) + 1e-06)
    normed = residual * spread * gain_ref[...].astype(jnp.float32)
    residual_ref[...] = residual.reshape(rows, parts, LANES)
    rows32[...] = normed.astype(jnp.bfloat16).reshape(rows, parts, LANES)
    out_ref[...] = jnp.zeros_like(out_ref)

    def one(t, _):
        row = rows32[t]
        for k in range(8):
            out_ref[place_ref[t * 8 + k]] = row
        return 0
    lax.fori_loop(0, rows, one, 0, unroll=8)

def pack(meta, place, attended, near, far, stream, gain, slots_count):
    rows, width = stream.shape
    parts = width // LANES
    return pl.pallas_call(
        pack_kernel,
        out_shape=(
            jax.ShapeDtypeStruct((rows, parts, LANES), jnp.float32),
            jax.ShapeDtypeStruct((slots_count, parts, LANES), jnp.bfloat16),
        ),
        in_specs=[SM, SM] + [VM] * 5,
        out_specs=(VM, VM),
        scratch_shapes=[pltpu.VMEM((rows, parts, LANES), jnp.bfloat16)],
        compiler_params=pltpu.CompilerParams(vmem_limit_bytes=32 << 20),
        name="pack",
    )(meta, place, attended, near, far, stream, gain)


TR = 384


def experts_kernel(x_ref, gate_ref, up_ref, down_ref, out_ref):
    rows, parts, lanes = x_ref.shape
    x = x_ref[...].reshape(rows, parts * lanes)
    gate = jnp.dot(x, gate_ref[0], preferred_element_type=jnp.float32)
    upper = jnp.dot(x, up_ref[0], preferred_element_type=jnp.float32)
    hidden = (gate / (1.0 + jnp.exp(-gate)) * upper).astype(jnp.bfloat16)
    result = jnp.dot(hidden, down_ref[0], preferred_element_type=jnp.float32)
    out_ref[...] = result.astype(jnp.bfloat16).reshape(rows, parts, lanes)


def experts(x, gate, up, down):
    count, parts, lanes = x.shape
    return pl.pallas_call(
        experts_kernel,
        out_shape=jax.ShapeDtypeStruct(x.shape, jnp.bfloat16),
        grid=(count // TR,),
        in_specs=[
            pl.BlockSpec((TR, parts, lanes), lambda i: (i, 0, 0)),
            VM,
            VM,
            VM,
        ],
        out_specs=pl.BlockSpec((TR, parts, lanes), lambda i: (i, 0, 0)),
        compiler_params=pltpu.CompilerParams(vmem_limit_bytes=36 << 20),
        name="experts",
    )(x, gate, up, down)


def combine_kernel(place_ref, shares_ref, residual_ref, back_ref, out_ref, total):
    rows, parts, lanes = residual_ref.shape
    def one(t, _):
        acc = residual_ref[t]
        for k in range(8):
            acc = acc + shares_ref[t * 8 + k] * back_ref[place_ref[t * 8 + k]].astype(jnp.float32)
        total[t] = acc.astype(jnp.bfloat16)
        return 0
    lax.fori_loop(0, rows, one, 0, unroll=8)
    out_ref[...] = total[...].reshape(rows, parts * lanes)

def combine(place, shares, residual, back):
    rows, parts, lanes = residual.shape
    return pl.pallas_call(
        combine_kernel,
        out_shape=jax.ShapeDtypeStruct((rows, parts * lanes), jnp.bfloat16),
        in_specs=[SM, SM, VM, VM], out_specs=VM,
        scratch_shapes=[pltpu.VMEM((rows, parts, lanes), jnp.bfloat16)],
        compiler_params=pltpu.CompilerParams(vmem_limit_bytes=48 << 20),
        name="combine",
    )(place, shares, residual, back)


def permute(x, move):
    pairs = []
    for n in range(128):
        ctx, exp = divmod(n, 8)
        x_lo, z, core = ctx // 8, ctx // 2 % 4, ctx % 2
        y, x_hi = exp // 2, exp % 2
        target = move(x_hi * 2 + x_lo, y, z, core)
        if target is None:
            continue
        tx, ty, tz, tc = target
        tx, ty, tz = tx % 4, ty % 4, tz % 4
        pairs.append((n, ((tx % 2) * 8 + tz * 2 + tc) * 8 + ty * 2 + tx // 2))
    return lax.ppermute(x, ("ctx", "exp"), pairs)


def along_z(a, step):
    return permute(a, lambda x, y, z, c: (x, y, z + step, c))


def along_y(a, step):
    return permute(a, lambda x, y, z, c: (x, y + step, z, c))


def other_core(a):
    return permute(a, lambda x, y, z, c: (x, y, z, 1 - c))


def down_x(a, step):
    return permute(a, lambda x, y, z, c: (x + step, y, z, c) if x % 2 == 1 else None)


def back_x(a, step):
    return permute(a, lambda x, y, z, c: (x + step, y, z, c) if x % 2 == 0 else None)


def on_device(
    stream,
    queries,
    keys,
    values,
    out_proj,
    norm_gain,
    gate_proj,
    up_proj,
    down_proj,
    expert_ids,
    route_weights,
    segment_lengths,
):
    ctx_count = lax.axis_size("ctx")
    exp_count = lax.axis_size("exp")
    ctx_index = lax.axis_index("ctx").astype(jnp.int32)
    exp_index = lax.axis_index("exp").astype(jnp.int32)
    rows_ctx = queries.shape[0]
    expert_count = ctx_count * exp_count
    tok_rows, top_count = expert_ids.shape
    capacity = max(2, tok_rows * top_count * 9 // (expert_count * 8))
    core = ctx_index % 2
    y = exp_index // 2
    own = jnp.concatenate(
        [lax.dynamic_slice_in_dim(keys, y * HD, HD, 1), lax.dynamic_slice_in_dim(values, y * HD, HD, 1)],
        axis=1,
    )
    own, out_proj = lax.optimization_barrier((own, out_proj))
    middle = rows_ctx // 2
    up, down = along_z(own, 1), along_z(own, -1)
    q_sent = (down_x(queries[:middle], -1), down_x(queries[middle:], 1))
    far_a, far_b = along_z(up[:middle], 1), along_z(down[middle:], -1)
    near = (own, up, down, far_a, far_b)
    pieces = near + tuple(other_core(piece) for piece in near)

    mine = lax.dynamic_slice_in_dim(out_proj, core * LANES, LANES, 0)
    w_near = lax.all_gather(mine, "exp", axis=0, tiled=True)

    place, shares = slots(expert_ids, route_weights, capacity)
    place = place.reshape(-1)
    shares = shares.reshape(-1)

    here = ctx_index.reshape(1)
    sent = attend(False, here, segment_lengths, q_sent, pieces, 4)
    here, first, second = lax.optimization_barrier((here, *sent))
    first, second = back_x(first, 1), back_x(second, -1)
    own_parts = attend(True, here, segment_lengths, (queries,), pieces, 5)
    attended = merge(here, (first, second), own_parts)
    w_ready, _ = lax.optimization_barrier((w_near, attended))
    w_far = other_core(w_ready)
    spread = lax.all_to_all(
        attended.reshape(exp_count, tok_rows, 2 * HD), "exp", split_axis=0, concat_axis=0, tiled=True
    )
    residual, outgoing = pack(
        here,
        place,
        spread,
        w_ready,
        w_far,
        stream,
        norm_gain.reshape(1, -1),
        expert_count * capacity,
    )
    shape = (expert_count, capacity) + outgoing.shape[1:]
    arrived = lax.all_to_all(
        outgoing.reshape(shape), ("ctx", "exp"), split_axis=0, concat_axis=0, tiled=True
    )
    results = experts(arrived.reshape(outgoing.shape), gate_proj, up_proj, down_proj)
    returned = lax.all_to_all(
        results.reshape(shape), ("ctx", "exp"), split_axis=0, concat_axis=0, tiled=True
    )
    return combine(place, shares, residual, returned.reshape(outgoing.shape))


def solution(mesh):
    placed = (
        P(("ctx", "exp"), None),
        P("ctx", "exp"),
        P("ctx", None),
        P("ctx", None),
        P("exp", None),
        P(),
        P(("ctx", "exp"), None, None),
        P(("ctx", "exp"), None, None),
        P(("ctx", "exp"), None, None),
        P(("ctx", "exp"), None),
        P(("ctx", "exp"), None),
        P(),
    )
    return jax.shard_map(
        on_device, mesh=mesh, in_specs=placed, out_specs=P(("ctx", "exp"), None), check_vma=False
    )
```

```python
import functools
import math

import jax
import jax.numpy as jnp
from jax import lax
from jax.experimental import pallas as pl
from jax.experimental.pallas import tpu as pltpu
from jax.sharding import PartitionSpec as P

HD = 128
KVH = 4
HQ = 16
LANES = 128
SEGMENTS = 17
SHARD = 1024
HALF = 8
TQ = 1024
RC = 256
NEVER = -1e30
VM = pl.BlockSpec(memory_space=pltpu.VMEM)
SM = pl.BlockSpec(memory_space=pltpu.SMEM)
HBM = pl.BlockSpec(memory_space=pl.ANY)


def attend_part(final, meta_ref, lengths_ref, *refs):
    pieces = refs[:10]
    count_q = 1 if final else 2
    q_refs, out_refs = refs[10 : 10 + count_q], refs[10 + count_q : 12 + count_q]
    kv_s, q_s, m_s, acc_s, v_s, start_s, sems = refs[12 + count_q :]
    ctx = meta_ref[0]
    half, z, core = ctx // HALF, (ctx // 2) & 3, ctx & 1
    low = half * HALF
    if final:
        base, active = ctx * SHARD, jnp.int32(1)
    else:
        base, active = (ctx + HALF) * SHARD, 1 - half
    prompt = lengths_ref[0]
    scale = math.log2(math.e) / math.sqrt(HD)

    first = base
    begin = jnp.int32(0)
    begin_last = jnp.int32(0)
    end = jnp.int32(0)
    for s in range(SEGMENTS):
        end = end + lengths_ref[s]
        begin = jnp.where(first >= end, end, begin)
        begin_last = jnp.where(first + TQ - 1 >= end, end, begin_last)
    last = (first + TQ - 1) // SHARD
    shared = jnp.minimum((prompt + SHARD - 1) // SHARD, last + 1)
    own = jnp.maximum(begin // SHARD, shared)
    one_from, one_to = low, jnp.minimum(shared, low + HALF)
    two_from, two_to = jnp.maximum(own, low), jnp.minimum(last + 1, low + HALF)
    one_count = jnp.maximum(one_to - one_from, 0)
    count = one_count + jnp.maximum(two_to - two_from, 0)

    copies = []
    for other in range(2):
        side = core if other == 0 else 1 - core
        for n, (dz, begin_row) in enumerate(((0, 0), (3, 0), (1, 0), (2, 0), (2, SHARD // 2))):
            piece = pieces[other * 5 + n]
            shard = ((z + dz) & 3) * 2 + side
            target = kv_s.at[shard, pl.ds(begin_row, piece.shape[0])]
            number = low + shard
            used = (number < one_to) | ((number >= two_from) & (number < two_to))
            copies.append(
                ((active > 0) & used, pltpu.make_async_copy(piece, target, sems.at[other * 5 + n]))
            )

    for used, copy in copies:
        pl.when(used)(copy.start)

    @pl.when(active > 0)
    def _():
        v_s[:, HD:] = jnp.ones((SHARD, HD), jnp.bfloat16)
        pos = first + lax.broadcasted_iota(jnp.int32, (TQ, LANES), 0)
        starts = jnp.zeros_like(pos)
        end = jnp.int32(0)
        for i in range(SEGMENTS):
            end = end + lengths_ref[i]
            starts = jnp.where(pos >= end, end, starts)
        start_s[...] = starts
        for head in range(2):
            hs = slice(head * HD, (head + 1) * HD)
            q = jnp.concatenate([ref[:, hs] for ref in q_refs], axis=0).astype(jnp.float32) * scale
            rounded = q.astype(jnp.bfloat16)
            q_s[head * TQ : (head + 1) * TQ, :HD] = rounded
            q_s[head * TQ : (head + 1) * TQ, HD:] = (q - rounded.astype(jnp.float32)).astype(jnp.bfloat16)
        m_s[...] = jnp.full_like(m_s, NEVER)
        acc_s[...] = jnp.zeros_like(acc_s)

    for used, copy in copies:
        pl.when(used)(copy.wait)

    @pl.when(active > 0)
    def _():
        def block(number, masked):
            lo = number * SHARD
            k = kv_s[number - low, :, :HD]
            k = jnp.concatenate([k, k], axis=1)
            v_s[:, :HD] = kv_s[number - low, :, HD:]
            v = v_s[...]

            def score(r):
                return lax.dot_general(
                    q_s[pl.ds(r * RC, RC)], k, (((1,), (1,)), ((), ())), preferred_element_type=jnp.float32
                )

            ahead = score(0)
            for r in range(2 * TQ // RC):
                rs = pl.ds(r * RC, RC)
                s = ahead
                if r + 1 < 2 * TQ // RC:
                    ahead = score(r + 1)
                if masked:
                    pos = first + (r * RC) % TQ + lax.broadcasted_iota(jnp.int32, (RC, 1), 0)
                    starts = start_s[pl.ds((r * RC) % TQ, RC)][:, :1]
                    kpos = lo + lax.broadcasted_iota(jnp.int32, (1, SHARD), 1)
                    seen = jnp.where(kpos < prompt, SHARD * 2 * HALF, kpos) >= starts
                    if final:
                        seen = seen & (kpos <= pos)
                    s = jnp.where(seen, s, NEVER)
                old = m_s[rs]
                new = jnp.maximum(old, jnp.max(s, axis=1, keepdims=True))
                p = jnp.exp2(s - new[:, :1]).astype(jnp.bfloat16)
                m_s[rs] = new
                alpha = jnp.exp2(old - new)
                pv = jnp.dot(p, v, preferred_element_type=jnp.float32)
                acc_s[rs, :HD] = acc_s[rs, :HD] * alpha + pv[:, :HD]
                acc_s[rs, HD:] = acc_s[rs, HD:] * alpha + pv[:, HD:]

        def step(i, _):
            number = jnp.where(i < one_count, one_from + i, two_from + i - one_count)
            lo = number * SHARD
            hi = lo + SHARD
            whole = (hi <= first + 1) & ((hi <= prompt) | (lo >= begin_last))
            pl.when(whole)(lambda: block(number, False))
            pl.when(jnp.logical_not(whole))(lambda: block(number, True))
            return 0

        lax.fori_loop(0, count, step, 0)
        rows, terms = TQ // 2, []
        for head in range(2):
            hs = pl.ds(head * TQ, TQ)
            total = acc_s[hs, HD:]
            o = acc_s[hs, :HD] / total
            lse = m_s[hs] + jnp.log2(total)
            a = lse.astype(jnp.bfloat16).astype(jnp.float32)
            b = (lse - a).astype(jnp.bfloat16).astype(jnp.float32)
            terms += [a, b, lse - a - b]
            o = o.astype(jnp.bfloat16)
            for n in range(2):
                out_refs[n][:, head * HD : (head + 1) * HD] = o[n * rows : (n + 1) * rows]
        lane = lax.broadcasted_iota(jnp.int32, (TQ, LANES), 1)
        parts = terms[-1]
        for n in range(len(terms) - 1):
            parts = jnp.where(lane == n, terms[n], parts)
        parts = parts.astype(jnp.bfloat16)
        for n in range(2):
            out_refs[n][:, 2 * HD :] = parts[n * rows : (n + 1) * rows]


def attend(final, meta, lengths, q, pieces, blocks):
    shapes = tuple(jax.ShapeDtypeStruct((TQ // 2, 2 * HD + LANES), jnp.bfloat16) for _ in range(2))
    return pl.pallas_call(
        functools.partial(attend_part, final),
        out_shape=shapes,
        in_specs=[SM, SM] + [HBM] * 10 + [VM] * len(q),
        out_specs=(VM, VM),
        scratch_shapes=[
            pltpu.VMEM((HALF, SHARD, 2 * HD), jnp.bfloat16),
            pltpu.VMEM((2 * TQ, 2 * HD), jnp.bfloat16),
            pltpu.VMEM((2 * TQ, HD), jnp.float32),
            pltpu.VMEM((2 * TQ, 2 * HD), jnp.float32),
            pltpu.VMEM((SHARD, 2 * HD), jnp.bfloat16),
            pltpu.VMEM((TQ, LANES), jnp.int32),
            pltpu.SemaphoreType.DMA((10,)),
        ],
        compiler_params=pltpu.CompilerParams(vmem_limit_bytes=57 << 20),
        cost_estimate=pl.CostEstimate(
            flops=blocks * 32 * HD * SHARD * SHARD, bytes_accessed=8 << 20, transcendentals=blocks * 2 * SHARD * SHARD
        ),
        name="attend_own" if final else "attend_sent",
    )(meta, lengths, *pieces, *q)


def merge_kernel(meta_ref, *refs):
    sent_refs, own_refs, out_ref = refs[:2], refs[2:4], refs[4]
    high = meta_ref[0] >= HALF
    half = out_ref.shape[0] // 2
    for n in range(2):
        sent_ref, own_ref = sent_refs[n], own_refs[n]
        for head in range(2):
            hs = slice(head * HD, (head + 1) * HD)

            def log_sum(ref):
                parts = ref[:, 2 * HD :].astype(jnp.float32)
                at = 3 * head
                return parts[:, at : at + 1] + parts[:, at + 1 : at + 2] + parts[:, at + 2 : at + 3]

            sent, here = jnp.where(high, log_sum(sent_ref), NEVER), log_sum(own_ref)
            top = jnp.maximum(sent, here)
            w_sent, w_here = jnp.exp2(sent - top), jnp.exp2(here - top)
            share = w_sent / (w_sent + w_here)
            a, b = sent_ref[:, hs].astype(jnp.float32), own_ref[:, hs].astype(jnp.float32)
            o = share * a + (1.0 - share) * b
            out_ref[n * half : (n + 1) * half, hs] = o.astype(jnp.bfloat16)


def merge(meta, sent, own):
    half = own[0].shape[0]
    return pl.pallas_call(
        merge_kernel,
        out_shape=jax.ShapeDtypeStruct((2 * half, 2 * HD), jnp.bfloat16),
        in_specs=[SM] + [VM] * 4,
        out_specs=VM,
        compiler_params=pltpu.CompilerParams(vmem_limit_bytes=16 << 20),
        name="merge",
    )(meta, *sent, *own)


def slots_kernel(capacity, ids_ref, weights_ref, place_ref, shares_ref):
    rows, top = ids_ref.shape
    experts = 128
    ids = ids_ref[...]
    lane = lax.broadcasted_iota(jnp.int32, (rows, experts), 1)
    named = [(ids[:, k : k + 1] == lane).astype(jnp.float32) for k in range(top)]
    chosen = functools.reduce(jnp.add, named).astype(jnp.bfloat16)
    before = (
        lax.broadcasted_iota(jnp.int32, (rows, rows), 1)
        < lax.broadcasted_iota(jnp.int32, (rows, rows), 0)
    ).astype(jnp.bfloat16)
    rank = jnp.dot(before, chosen, preferred_element_type=jnp.float32)
    slot = [jnp.sum(one * rank, axis=1, keepdims=True) for one in named]
    place_ref[...] = ids * capacity + jnp.concatenate(slot, axis=1).astype(jnp.int32)
    weights = weights_ref[...]
    shares_ref[...] = weights / jnp.sum(weights, axis=1, keepdims=True)

def slots(ids, weights, capacity):
    return pl.pallas_call(
        functools.partial(slots_kernel, capacity),
        out_shape=(jax.ShapeDtypeStruct(ids.shape, jnp.int32), jax.ShapeDtypeStruct(weights.shape, jnp.float32)),
        in_specs=[VM, VM], out_specs=(VM, VM), name="slots",
    )(ids, weights)

def pack_kernel(
    meta_ref, place_ref, attended_ref, near_ref, far_ref, stream_ref, gain_ref, residual_ref, out_ref, rows32
):
    rows, width = stream_ref.shape
    parts = width // LANES
    upper = (meta_ref[0] & 1) > 0
    near, far = [], []
    for e in range(attended_ref.shape[0]):
        a, b = attended_ref[e, :, :LANES], attended_ref[e, :, LANES:]
        near.append(jnp.where(upper, b, a))
        far.append(jnp.where(upper, a, b))
    projected = jnp.dot(
        jnp.concatenate(near, axis=1), near_ref[...], preferred_element_type=jnp.float32
    ) + jnp.dot(jnp.concatenate(far, axis=1), far_ref[...], preferred_element_type=jnp.float32)
    residual = stream_ref[...].astype(jnp.float32) + projected
    spread = lax.rsqrt(jnp.mean(residual * residual, axis=1, keepdims=True) + 1e-06)
    normed = residual * spread * gain_ref[...].astype(jnp.float32)
    residual_ref[...] = residual.reshape(rows, parts, LANES)
    rows32[...] = normed.astype(jnp.bfloat16).reshape(rows, parts, LANES)
    out_ref[...] = jnp.zeros_like(out_ref)

    def one(t, _):
        row = rows32[t]
        for k in range(8):
            out_ref[place_ref[t * 8 + k]] = row
        return 0
    lax.fori_loop(0, rows, one, 0, unroll=8)

def pack(meta, place, attended, near, far, stream, gain, slots_count):
    rows, width = stream.shape
    parts = width // LANES
    return pl.pallas_call(
        pack_kernel,
        out_shape=(
            jax.ShapeDtypeStruct((rows, parts, LANES), jnp.float32),
            jax.ShapeDtypeStruct((slots_count, parts, LANES), jnp.bfloat16),
        ),
        in_specs=[SM, SM] + [VM] * 5,
        out_specs=(VM, VM),
        scratch_shapes=[pltpu.VMEM((rows, parts, LANES), jnp.bfloat16)],
        compiler_params=pltpu.CompilerParams(vmem_limit_bytes=32 << 20),
        name="pack",
    )(meta, place, attended, near, far, stream, gain)


TR = 384


def experts_kernel(x_ref, gate_ref, up_ref, down_ref, out_ref):
    rows, parts, lanes = x_ref.shape
    x = x_ref[...].reshape(rows, parts * lanes)
    gate = jnp.dot(x, gate_ref[0], preferred_element_type=jnp.float32)
    upper = jnp.dot(x, up_ref[0], preferred_element_type=jnp.float32)
    hidden = (gate / (1.0 + jnp.exp(-gate)) * upper).astype(jnp.bfloat16)
    result = jnp.dot(hidden, down_ref[0], preferred_element_type=jnp.float32)
    out_ref[...] = result.astype(jnp.bfloat16).reshape(rows, parts, lanes)


def experts(x, gate, up, down):
    count, parts, lanes = x.shape
    return pl.pallas_call(
        experts_kernel,
        out_shape=jax.ShapeDtypeStruct(x.shape, jnp.bfloat16),
        grid=(count // TR,),
        in_specs=[
            pl.BlockSpec((TR, parts, lanes), lambda i: (i, 0, 0)),
            VM,
            VM,
            VM,
        ],
        out_specs=pl.BlockSpec((TR, parts, lanes), lambda i: (i, 0, 0)),
        compiler_params=pltpu.CompilerParams(vmem_limit_bytes=36 << 20),
        name="experts",
    )(x, gate, up, down)


def combine_kernel(place_ref, shares_ref, residual_ref, back_ref, out_ref, total):
    rows, parts, lanes = residual_ref.shape
    def one(t, _):
        acc = residual_ref[t]
        for k in range(8):
            acc = acc + shares_ref[t * 8 + k] * back_ref[place_ref[t * 8 + k]].astype(jnp.float32)
        total[t] = acc.astype(jnp.bfloat16)
        return 0
    lax.fori_loop(0, rows, one, 0, unroll=8)
    out_ref[...] = total[...].reshape(rows, parts * lanes)

def combine(place, shares, residual, back):
    rows, parts, lanes = residual.shape
    return pl.pallas_call(
        combine_kernel,
        out_shape=jax.ShapeDtypeStruct((rows, parts * lanes), jnp.bfloat16),
        in_specs=[SM, SM, VM, VM], out_specs=VM,
        scratch_shapes=[pltpu.VMEM((rows, parts, lanes), jnp.bfloat16)],
        compiler_params=pltpu.CompilerParams(vmem_limit_bytes=48 << 20),
        name="combine",
    )(place, shares, residual, back)


def permute(x, move):
    pairs = []
    for n in range(128):
        ctx, exp = divmod(n, 8)
        x_lo, z, core = ctx // 8, ctx // 2 % 4, ctx % 2
        y, x_hi = exp // 2, exp % 2
        target = move(x_hi * 2 + x_lo, y, z, core)
        if target is None:
            continue
        tx, ty, tz, tc = target
        tx, ty, tz = tx % 4, ty % 4, tz % 4
        pairs.append((n, ((tx % 2) * 8 + tz * 2 + tc) * 8 + ty * 2 + tx // 2))
    return lax.ppermute(x, ("ctx", "exp"), pairs)


def along_z(a, step):
    return permute(a, lambda x, y, z, c: (x, y, z + step, c))


def along_y(a, step):
    return permute(a, lambda x, y, z, c: (x, y + step, z, c))


def other_core(a):
    return permute(a, lambda x, y, z, c: (x, y, z, 1 - c))


def down_x(a, step):
    return permute(a, lambda x, y, z, c: (x + step, y, z, c) if x % 2 == 1 else None)


def back_x(a, step):
    return permute(a, lambda x, y, z, c: (x + step, y, z, c) if x % 2 == 0 else None)


def on_device(
    stream,
    queries,
    keys,
    values,
    out_proj,
    norm_gain,
    gate_proj,
    up_proj,
    down_proj,
    expert_ids,
    route_weights,
    segment_lengths,
):
    ctx_count = lax.axis_size("ctx")
    exp_count = lax.axis_size("exp")
    ctx_index = lax.axis_index("ctx").astype(jnp.int32)
    exp_index = lax.axis_index("exp").astype(jnp.int32)
    rows_ctx = queries.shape[0]
    expert_count = ctx_count * exp_count
    tok_rows, top_count = expert_ids.shape
    capacity = max(2, tok_rows * top_count * 9 // (expert_count * 8))
    core = ctx_index % 2
    y = exp_index // 2
    own = jnp.concatenate(
        [lax.dynamic_slice_in_dim(keys, y * HD, HD, 1), lax.dynamic_slice_in_dim(values, y * HD, HD, 1)],
        axis=1,
    )
    own, out_proj = lax.optimization_barrier((own, out_proj))
    middle = rows_ctx // 2
    up, down = along_z(own, 1), along_z(own, -1)
    q_sent = (down_x(queries[:middle], -1), down_x(queries[middle:], 1))
    far_a, far_b = along_z(up[:middle], 1), along_z(down[middle:], -1)
    near = (own, up, down, far_a, far_b)
    pieces = near + tuple(other_core(piece) for piece in near)

    mine = lax.dynamic_slice_in_dim(out_proj, core * LANES, LANES, 0)
    w_near = lax.all_gather(mine, "exp", axis=0, tiled=True)

    place, shares = slots(expert_ids, route_weights, capacity)
    place = place.reshape(-1)
    shares = shares.reshape(-1)

    here = ctx_index.reshape(1)
    sent = attend(False, here, segment_lengths, q_sent, pieces, 4)
    here, first, second = lax.optimization_barrier((here, *sent))
    first, second = back_x(first, 1), back_x(second, -1)
    own_parts = attend(True, here, segment_lengths, (queries,), pieces, 5)
    attended = merge(here, (first, second), own_parts)
    w_ready, _ = lax.optimization_barrier((w_near, attended))
    w_far = other_core(w_ready)
    spread = lax.all_to_all(
        attended.reshape(exp_count, tok_rows, 2 * HD), "exp", split_axis=0, concat_axis=0, tiled=True
    )
    residual, outgoing = pack(
        here,
        place,
        spread,
        w_ready,
        w_far,
        stream,
        norm_gain.reshape(1, -1),
        expert_count * capacity,
    )
    shape = (expert_count, capacity) + outgoing.shape[1:]
    arrived = lax.all_to_all(
        outgoing.reshape(shape), ("ctx", "exp"), split_axis=0, concat_axis=0, tiled=True
    )
    results = experts(arrived.reshape(outgoing.shape), gate_proj, up_proj, down_proj)
    returned = lax.all_to_all(
        results.reshape(shape), ("ctx", "exp"), split_axis=0, concat_axis=0, tiled=True
    )
    return combine(place, shares, residual, returned.reshape(outgoing.shape))


def solution(mesh):
    placed = (
        P(("ctx", "exp"), None),
        P("ctx", "exp"),
        P("ctx", None),
        P("ctx", None),
        P("exp", None),
        P(),
        P(("ctx", "exp"), None, None),
        P(("ctx", "exp"), None, None),
        P(("ctx", "exp"), None, None),
        P(("ctx", "exp"), None),
        P(("ctx", "exp"), None),
        P(),
    )
    return jax.shard_map(
        on_device, mesh=mesh, in_specs=placed, out_specs=P(("ctx", "exp"), None), check_vma=False
    )
```

```python
import functools
import math

import jax
import jax.numpy as jnp
from jax import lax
from jax.experimental import pallas as pl
from jax.experimental.pallas import tpu as pltpu
from jax.sharding import PartitionSpec as P

HD = 128
KVH = 4
HQ = 16
LANES = 128
SEGMENTS = 17
SHARD = 1024
HALF = 8
TQ = 1024
RC = 256
NEVER = -1e30
VM = pl.BlockSpec(memory_space=pltpu.VMEM)
SM = pl.BlockSpec(memory_space=pltpu.SMEM)
HBM = pl.BlockSpec(memory_space=pl.ANY)


def attend_part(final, meta_ref, lengths_ref, *refs):
    pieces = refs[:10]
    count_q = 1 if final else 2
    q_refs, out_refs = refs[10 : 10 + count_q], refs[10 + count_q : 12 + count_q]
    kv_s, q_s, m_s, acc_s, v_s, start_s, sems = refs[12 + count_q :]
    ctx = meta_ref[0]
    half, z, core = ctx // HALF, (ctx // 2) & 3, ctx & 1
    low = half * HALF
    if final:
        base, active = ctx * SHARD, jnp.int32(1)
    else:
        base, active = (ctx + HALF) * SHARD, 1 - half
    prompt = lengths_ref[0]
    scale = math.log2(math.e) / math.sqrt(HD)

    first = base
    begin = jnp.int32(0)
    begin_last = jnp.int32(0)
    end = jnp.int32(0)
    for s in range(SEGMENTS):
        end = end + lengths_ref[s]
        begin = jnp.where(first >= end, end, begin)
        begin_last = jnp.where(first + TQ - 1 >= end, end, begin_last)
    last = (first + TQ - 1) // SHARD
    shared = jnp.minimum((prompt + SHARD - 1) // SHARD, last + 1)
    own = jnp.maximum(begin // SHARD, shared)
    one_from, one_to = low, jnp.minimum(shared, low + HALF)
    two_from, two_to = jnp.maximum(own, low), jnp.minimum(last + 1, low + HALF)
    one_count = jnp.maximum(one_to - one_from, 0)
    count = one_count + jnp.maximum(two_to - two_from, 0)

    copies = []
    for other in range(2):
        side = core if other == 0 else 1 - core
        for n, (dz, begin_row) in enumerate(((0, 0), (3, 0), (1, 0), (2, 0), (2, SHARD // 2))):
            piece = pieces[other * 5 + n]
            shard = ((z + dz) & 3) * 2 + side
            target = kv_s.at[shard, pl.ds(begin_row, piece.shape[0])]
            number = low + shard
            used = (number < one_to) | ((number >= two_from) & (number < two_to))
            copies.append(
                ((active > 0) & used, pltpu.make_async_copy(piece, target, sems.at[other * 5 + n]))
            )

    for used, copy in copies:
        pl.when(used)(copy.start)

    @pl.when(active > 0)
    def _():
        v_s[:, HD:] = jnp.ones((SHARD, HD), jnp.bfloat16)
        pos = first + lax.broadcasted_iota(jnp.int32, (TQ, LANES), 0)
        starts = jnp.zeros_like(pos)
        end = jnp.int32(0)
        for i in range(SEGMENTS):
            end = end + lengths_ref[i]
            starts = jnp.where(pos >= end, end, starts)
        start_s[...] = starts
        for head in range(2):
            hs = slice(head * HD, (head + 1) * HD)
            q = jnp.concatenate([ref[:, hs] for ref in q_refs], axis=0).astype(jnp.float32) * scale
            rounded = q.astype(jnp.bfloat16)
            q_s[head * TQ : (head + 1) * TQ, :HD] = rounded
            q_s[head * TQ : (head + 1) * TQ, HD:] = (q - rounded.astype(jnp.float32)).astype(jnp.bfloat16)
        m_s[...] = jnp.full_like(m_s, NEVER)
        acc_s[...] = jnp.zeros_like(acc_s)

    for used, copy in copies:
        pl.when(used)(copy.wait)

    @pl.when(active > 0)
    def _():
        def block(number, masked):
            lo = number * SHARD
            k = kv_s[number - low, :, :HD]
            k = jnp.concatenate([k, k], axis=1)
            v_s[:, :HD] = kv_s[number - low, :, HD:]
            v = v_s[...]

            def score(r):
                return lax.dot_general(
                    q_s[pl.ds(r * RC, RC)], k, (((1,), (1,)), ((), ())), preferred_element_type=jnp.float32
                )

            ahead = score(0)
            for r in range(2 * TQ // RC):
                rs = pl.ds(r * RC, RC)
                s = ahead
                if r + 1 < 2 * TQ // RC:
                    ahead = score(r + 1)
                if masked:
                    pos = first + (r * RC) % TQ + lax.broadcasted_iota(jnp.int32, (RC, 1), 0)
                    starts = start_s[pl.ds((r * RC) % TQ, RC)][:, :1]
                    kpos = lo + lax.broadcasted_iota(jnp.int32, (1, SHARD), 1)
                    seen = jnp.where(kpos < prompt, SHARD * 2 * HALF, kpos) >= starts
                    if final:
                        seen = seen & (kpos <= pos)
                    s = jnp.where(seen, s, NEVER)
                old = m_s[rs]
                new = jnp.maximum(old, jnp.max(s, axis=1, keepdims=True))
                p = jnp.exp2(s - new[:, :1]).astype(jnp.bfloat16)
                m_s[rs] = new
                alpha = jnp.exp2(old - new)
                pv = jnp.dot(p, v, preferred_element_type=jnp.float32)
                acc_s[rs, :HD] = acc_s[rs, :HD] * alpha + pv[:, :HD]
                acc_s[rs, HD:] = acc_s[rs, HD:] * alpha + pv[:, HD:]

        def step(i, _):
            number = jnp.where(i < one_count, one_from + i, two_from + i - one_count)
            lo = number * SHARD
            hi = lo + SHARD
            whole = (hi <= first + 1) & ((hi <= prompt) | (lo >= begin_last))
            pl.when(whole)(lambda: block(number, False))
            pl.when(jnp.logical_not(whole))(lambda: block(number, True))
            return 0

        lax.fori_loop(0, count, step, 0)
        rows, terms = TQ // 2, []
        for head in range(2):
            hs = pl.ds(head * TQ, TQ)
            total = acc_s[hs, HD:]
            o = acc_s[hs, :HD] / total
            lse = m_s[hs] + jnp.log2(total)
            a = lse.astype(jnp.bfloat16).astype(jnp.float32)
            b = (lse - a).astype(jnp.bfloat16).astype(jnp.float32)
            terms += [a, b, lse - a - b]
            o = o.astype(jnp.bfloat16)
            for n in range(2):
                out_refs[n][:, head * HD : (head + 1) * HD] = o[n * rows : (n + 1) * rows]
        lane = lax.broadcasted_iota(jnp.int32, (TQ, LANES), 1)
        parts = terms[-1]
        for n in range(len(terms) - 1):
            parts = jnp.where(lane == n, terms[n], parts)
        parts = parts.astype(jnp.bfloat16)
        for n in range(2):
            out_refs[n][:, 2 * HD :] = parts[n * rows : (n + 1) * rows]


def attend(final, meta, lengths, q, pieces, blocks):
    shapes = tuple(jax.ShapeDtypeStruct((TQ // 2, 2 * HD + LANES), jnp.bfloat16) for _ in range(2))
    return pl.pallas_call(
        functools.partial(attend_part, final),
        out_shape=shapes,
        in_specs=[SM, SM] + [HBM] * 10 + [VM] * len(q),
        out_specs=(VM, VM),
        scratch_shapes=[
            pltpu.VMEM((HALF, SHARD, 2 * HD), jnp.bfloat16),
            pltpu.VMEM((2 * TQ, 2 * HD), jnp.bfloat16),
            pltpu.VMEM((2 * TQ, HD), jnp.float32),
            pltpu.VMEM((2 * TQ, 2 * HD), jnp.float32),
            pltpu.VMEM((SHARD, 2 * HD), jnp.bfloat16),
            pltpu.VMEM((TQ, LANES), jnp.int32),
            pltpu.SemaphoreType.DMA((10,)),
        ],
        compiler_params=pltpu.CompilerParams(vmem_limit_bytes=57 << 20),
        cost_estimate=pl.CostEstimate(
            flops=blocks * 32 * HD * SHARD * SHARD, bytes_accessed=8 << 20, transcendentals=blocks * 2 * SHARD * SHARD
        ),
        name="attend_own" if final else "attend_sent",
    )(meta, lengths, *pieces, *q)


def merge_kernel(meta_ref, *refs):
    sent_refs, own_refs, out_ref = refs[:2], refs[2:4], refs[4]
    high = meta_ref[0] >= HALF
    half = out_ref.shape[0] // 2
    for n in range(2):
        sent_ref, own_ref = sent_refs[n], own_refs[n]
        for head in range(2):
            hs = slice(head * HD, (head + 1) * HD)

            def log_sum(ref):
                parts = ref[:, 2 * HD :].astype(jnp.float32)
                at = 3 * head
                return parts[:, at : at + 1] + parts[:, at + 1 : at + 2] + parts[:, at + 2 : at + 3]

            sent, here = jnp.where(high, log_sum(sent_ref), NEVER), log_sum(own_ref)
            top = jnp.maximum(sent, here)
            w_sent, w_here = jnp.exp2(sent - top), jnp.exp2(here - top)
            share = w_sent / (w_sent + w_here)
            a, b = sent_ref[:, hs].astype(jnp.float32), own_ref[:, hs].astype(jnp.float32)
            o = share * a + (1.0 - share) * b
            out_ref[n * half : (n + 1) * half, hs] = o.astype(jnp.bfloat16)


def merge(meta, sent, own):
    half = own[0].shape[0]
    return pl.pallas_call(
        merge_kernel,
        out_shape=jax.ShapeDtypeStruct((2 * half, 2 * HD), jnp.bfloat16),
        in_specs=[SM] + [VM] * 4,
        out_specs=VM,
        compiler_params=pltpu.CompilerParams(vmem_limit_bytes=16 << 20),
        name="merge",
    )(meta, *sent, *own)


def slots_kernel(capacity, ids_ref, weights_ref, place_ref, shares_ref):
    rows, top = ids_ref.shape
    experts = 128
    ids = ids_ref[...]
    lane = lax.broadcasted_iota(jnp.int32, (rows, experts), 1)
    named = [(ids[:, k : k + 1] == lane).astype(jnp.float32) for k in range(top)]
    chosen = functools.reduce(jnp.add, named).astype(jnp.bfloat16)
    before = (
        lax.broadcasted_iota(jnp.int32, (rows, rows), 1)
        < lax.broadcasted_iota(jnp.int32, (rows, rows), 0)
    ).astype(jnp.bfloat16)
    rank = jnp.dot(before, chosen, preferred_element_type=jnp.float32)
    slot = [jnp.sum(one * rank, axis=1, keepdims=True) for one in named]
    place_ref[...] = ids * capacity + jnp.concatenate(slot, axis=1).astype(jnp.int32)
    weights = weights_ref[...]
    shares_ref[...] = weights / jnp.sum(weights, axis=1, keepdims=True)

def slots(ids, weights, capacity):
    return pl.pallas_call(
        functools.partial(slots_kernel, capacity),
        out_shape=(jax.ShapeDtypeStruct(ids.shape, jnp.int32), jax.ShapeDtypeStruct(weights.shape, jnp.float32)),
        in_specs=[VM, VM], out_specs=(VM, VM), name="slots",
    )(ids, weights)

def pack_kernel(
    meta_ref, place_ref, attended_ref, near_ref, far_ref, stream_ref, gain_ref, residual_ref, out_ref, rows32
):
    rows, width = stream_ref.shape
    parts = width // LANES
    upper = (meta_ref[0] & 1) > 0
    near, far = [], []
    for e in range(attended_ref.shape[0]):
        a, b = attended_ref[e, :, :LANES], attended_ref[e, :, LANES:]
        near.append(jnp.where(upper, b, a))
        far.append(jnp.where(upper, a, b))
    projected = jnp.dot(
        jnp.concatenate(near, axis=1), near_ref[...], preferred_element_type=jnp.float32
    ) + jnp.dot(jnp.concatenate(far, axis=1), far_ref[...], preferred_element_type=jnp.float32)
    residual = stream_ref[...].astype(jnp.float32) + projected
    spread = lax.rsqrt(jnp.mean(residual * residual, axis=1, keepdims=True) + 1e-06)
    normed = residual * spread * gain_ref[...].astype(jnp.float32)
    residual_ref[...] = residual.reshape(rows, parts, LANES)
    rows32[...] = normed.astype(jnp.bfloat16).reshape(rows, parts, LANES)
    out_ref[...] = jnp.zeros_like(out_ref)

    def one(t, _):
        row = rows32[t]
        for k in range(8):
            out_ref[place_ref[t * 8 + k]] = row
        return 0
    lax.fori_loop(0, rows, one, 0, unroll=8)

def pack(meta, place, attended, near, far, stream, gain, slots_count):
    rows, width = stream.shape
    parts = width // LANES
    return pl.pallas_call(
        pack_kernel,
        out_shape=(
            jax.ShapeDtypeStruct((rows, parts, LANES), jnp.float32),
            jax.ShapeDtypeStruct((slots_count, parts, LANES), jnp.bfloat16),
        ),
        in_specs=[SM, SM] + [VM] * 5,
        out_specs=(VM, VM),
        scratch_shapes=[pltpu.VMEM((rows, parts, LANES), jnp.bfloat16)],
        compiler_params=pltpu.CompilerParams(vmem_limit_bytes=54 << 20),
        name="pack",
    )(meta, place, attended, near, far, stream, gain)


TR = 384


def experts_kernel(x_ref, gate_ref, up_ref, down_ref, out_ref):
    rows, parts, lanes = x_ref.shape
    x = x_ref[...].reshape(rows, parts * lanes)
    gate = jnp.dot(x, gate_ref[0], preferred_element_type=jnp.float32)
    upper = jnp.dot(x, up_ref[0], preferred_element_type=jnp.float32)
    hidden = (gate / (1.0 + jnp.exp(-gate)) * upper).astype(jnp.bfloat16)
    result = jnp.dot(hidden, down_ref[0], preferred_element_type=jnp.float32)
    out_ref[...] = result.astype(jnp.bfloat16).reshape(rows, parts, lanes)


def experts(x, gate, up, down):
    count, parts, lanes = x.shape
    return pl.pallas_call(
        experts_kernel,
        out_shape=jax.ShapeDtypeStruct(x.shape, jnp.bfloat16),
        grid=(count // TR,),
        in_specs=[
            pl.BlockSpec((TR, parts, lanes), lambda i: (i, 0, 0)),
            VM,
            VM,
            VM,
        ],
        out_specs=pl.BlockSpec((TR, parts, lanes), lambda i: (i, 0, 0)),
        compiler_params=pltpu.CompilerParams(vmem_limit_bytes=36 << 20),
        name="experts",
    )(x, gate, up, down)


def combine_kernel(place_ref, shares_ref, residual_ref, back_ref, out_ref, total):
    rows, parts, lanes = residual_ref.shape
    def one(t, _):
        acc = residual_ref[t]
        for k in range(8):
            acc = acc + shares_ref[t * 8 + k] * back_ref[place_ref[t * 8 + k]].astype(jnp.float32)
        total[t] = acc.astype(jnp.bfloat16)
        return 0
    lax.fori_loop(0, rows, one, 0, unroll=8)
    out_ref[...] = total[...].reshape(rows, parts * lanes)

def combine(place, shares, residual, back):
    rows, parts, lanes = residual.shape
    return pl.pallas_call(
        combine_kernel,
        out_shape=jax.ShapeDtypeStruct((rows, parts * lanes), jnp.bfloat16),
        in_specs=[SM, SM, VM, VM], out_specs=VM,
        scratch_shapes=[pltpu.VMEM((rows, parts, lanes), jnp.bfloat16)],
        compiler_params=pltpu.CompilerParams(vmem_limit_bytes=48 << 20),
        name="combine",
    )(place, shares, residual, back)


def permute(x, move):
    pairs = []
    for n in range(128):
        ctx, exp = divmod(n, 8)
        x_lo, z, core = ctx // 8, ctx // 2 % 4, ctx % 2
        y, x_hi = exp // 2, exp % 2
        target = move(x_hi * 2 + x_lo, y, z, core)
        if target is None:
            continue
        tx, ty, tz, tc = target
        tx, ty, tz = tx % 4, ty % 4, tz % 4
        pairs.append((n, ((tx % 2) * 8 + tz * 2 + tc) * 8 + ty * 2 + tx // 2))
    return lax.ppermute(x, ("ctx", "exp"), pairs)


def along_z(a, step):
    return permute(a, lambda x, y, z, c: (x, y, z + step, c))


def along_y(a, step):
    return permute(a, lambda x, y, z, c: (x, y + step, z, c))


def other_core(a):
    return permute(a, lambda x, y, z, c: (x, y, z, 1 - c))


def down_x(a, step):
    return permute(a, lambda x, y, z, c: (x + step, y, z, c) if x % 2 == 1 else None)


def back_x(a, step):
    return permute(a, lambda x, y, z, c: (x + step, y, z, c) if x % 2 == 0 else None)


def on_device(
    stream,
    queries,
    keys,
    values,
    out_proj,
    norm_gain,
    gate_proj,
    up_proj,
    down_proj,
    expert_ids,
    route_weights,
    segment_lengths,
):
    ctx_count = lax.axis_size("ctx")
    exp_count = lax.axis_size("exp")
    ctx_index = lax.axis_index("ctx").astype(jnp.int32)
    exp_index = lax.axis_index("exp").astype(jnp.int32)
    rows_ctx = queries.shape[0]
    expert_count = ctx_count * exp_count
    tok_rows, top_count = expert_ids.shape
    capacity = max(2, tok_rows * top_count * 9 // (expert_count * 8))
    core = ctx_index % 2
    y = exp_index // 2
    own = jnp.concatenate(
        [lax.dynamic_slice_in_dim(keys, y * HD, HD, 1), lax.dynamic_slice_in_dim(values, y * HD, HD, 1)],
        axis=1,
    )
    own, out_proj = lax.optimization_barrier((own, out_proj))
    middle = rows_ctx // 2
    up, down = along_z(own, 1), along_z(own, -1)
    q_sent = (down_x(queries[:middle], -1), down_x(queries[middle:], 1))
    far_a, far_b = along_z(up[:middle], 1), along_z(down[middle:], -1)
    near = (own, up, down, far_a, far_b)
    pieces = near + tuple(other_core(piece) for piece in near)

    mine = lax.dynamic_slice_in_dim(out_proj, core * LANES, LANES, 0)
    w_near = lax.all_gather(mine, "exp", axis=0, tiled=True)

    place, shares = slots(expert_ids, route_weights, capacity)
    place = place.reshape(-1)
    shares = shares.reshape(-1)

    here = ctx_index.reshape(1)
    sent = attend(False, here, segment_lengths, q_sent, pieces, 4)
    here, first, second = lax.optimization_barrier((here, *sent))
    first, second = back_x(first, 1), back_x(second, -1)
    own_parts = attend(True, here, segment_lengths, (queries,), pieces, 5)
    attended = merge(here, (first, second), own_parts)
    w_ready, _ = lax.optimization_barrier((w_near, attended))
    w_far = other_core(w_ready)
    spread = lax.all_to_all(
        attended.reshape(exp_count, tok_rows, 2 * HD), "exp", split_axis=0, concat_axis=0, tiled=True
    )
    residual, outgoing = pack(
        here,
        place,
        spread,
        w_ready,
        w_far,
        stream,
        norm_gain.reshape(1, -1),
        expert_count * capacity,
    )
    shape = (expert_count, capacity) + outgoing.shape[1:]
    arrived = lax.all_to_all(
        outgoing.reshape(shape), ("ctx", "exp"), split_axis=0, concat_axis=0, tiled=True
    )
    results = experts(arrived.reshape(outgoing.shape), gate_proj, up_proj, down_proj)
    returned = lax.all_to_all(
        results.reshape(shape), ("ctx", "exp"), split_axis=0, concat_axis=0, tiled=True
    )
    return combine(place, shares, residual, returned.reshape(outgoing.shape))


def solution(mesh):
    placed = (
        P(("ctx", "exp"), None),
        P("ctx", "exp"),
        P("ctx", None),
        P("ctx", None),
        P("exp", None),
        P(),
        P(("ctx", "exp"), None, None),
        P(("ctx", "exp"), None, None),
        P(("ctx", "exp"), None, None),
        P(("ctx", "exp"), None),
        P(("ctx", "exp"), None),
        P(),
    )
    return jax.shard_map(
        on_device, mesh=mesh, in_specs=placed, out_specs=P(("ctx", "exp"), None), check_vma=False
    )
```
